32 devices in a mesh: dp: 8 (over y, x, core), tensor: 4 (over z).
Axes of the slice: x: 2, y: 2, z: 4, core: 2. Of those that a mesh axis runs over, the one named last changes fastest.
Arguments:
- hidden_rows: bfloat16 [256, 16, 8192], P('tensor', 'dp'), may hold values from -6 to 6
- norm_gain: float32 [8192], replicated, may hold values from 0.1 to 1.9
- w_query: bfloat16 [8192, 4096], P(None, 'tensor'), may hold values from -0.0625 to 0.0625
- w_key: bfloat16 [8192, 1024], P(None, 'tensor'), may hold values from -0.0625 to 0.0625
- w_value: bfloat16 [8192, 1024], P(None, 'tensor'), may hold values from -0.0625 to 0.0625
- w_out: bfloat16 [4096, 8192], P('tensor'), may hold values from -1.5 to 1.5
- cache_keys: bfloat16 [16, 2048, 1024], P('dp', None, 'tensor'), may hold values from -6 to 6
- cache_values: bfloat16 [16, 2048, 1024], P('dp', None, 'tensor'), may hold values from -6 to 6
- slot_of_request: int32 [16], replicated, may hold values from 0 to 15, as said below
- span_length: int32 [16], replicated, may hold values from 1 to 256, as said below
- prefix_length: int32 [16], replicated, may hold values from 1 to 2048, as said below
Outputs:
- attention_out: bfloat16 [256, 16, 8192], P('tensor', 'dp')
The draws below stay inside these ranges and needn't reach their ends.
Inputs may be any that keep to these rules, and one draw needn't show every extreme that they name: `slot_of_request`: a permutation of the slots 0 to 15; slot i lies on dp index i // 2, request r starts on dp index r // 2; there are 2 distinct numbers m, one of them 1, the same for every dp index, such that the 2 requests of dp index i have their slots on the dp indices i XOR m, one on each. `span_length`: some request uses all 256 new positions. `prefix_length`: some request has all 2048 cached positions.
All inputs are finite; a program needn't handle non-finite values.
Results may differ from the reference program's by a relative error of at most 0.019.
Values may be sent and summed in bfloat16 or wider, within the bound.
No kernel may reach another device: no remote copies, remote signals or barrier semaphores. Data moves between devices by JAX's collectives and lax.ppermute only.
A program may use at most 192 MiB of HBM per device.

```python
import jax
import jax.numpy as jnp
from jax import lax

D = 8192
HEADS = 32
KVH = 8
HD = 128
R_DEV = 2
SPAN = 256
PREFIX = 2048
REQUESTS = 16


def draw_slot_of_request(key, part):
    device_count = REQUESTS // R_DEV
    keys = jax.random.split(jax.random.fold_in(key, 101), 3)
    shuffled = jax.random.permutation(keys[0], device_count).astype(jnp.int32)
    where_one = jnp.argmax(shuffled == 1).astype(jnp.int32)
    shuffled = shuffled.at[where_one].set(shuffled[0]).at[0].set(1)
    dp_masks = shuffled[:R_DEV]
    slot_shift = jax.random.randint(keys[1], (device_count,), 0, R_DEV)
    request_shift = jax.random.randint(keys[2], (device_count,), 0, R_DEV)
    source_rows = jnp.arange(device_count, dtype=jnp.int32)[:, None]
    column = jnp.arange(R_DEV, dtype=jnp.int32)[None, :]
    target = jnp.bitwise_xor(source_rows, dp_masks[column])
    local_slot = (column + slot_shift[target]) % R_DEV
    local_request = (column + request_shift[source_rows]) % R_DEV
    request_index = (source_rows * R_DEV + local_request).reshape(-1)
    slot_index = (target * R_DEV + local_slot).reshape(-1)
    return jnp.zeros((REQUESTS,), jnp.int32).at[request_index].set(slot_index.astype(jnp.int32))


def draw_span_length(key, part):
    first_key, second_key = jax.random.split(jax.random.fold_in(key, 202))
    drawn = jax.random.randint(first_key, (REQUESTS,), 1, SPAN + 1)
    full_request = jax.random.randint(second_key, (), 0, REQUESTS)
    return drawn.at[full_request].set(SPAN).astype(jnp.int32)


def draw_prefix_length(key, part):
    first_key, second_key = jax.random.split(jax.random.fold_in(key, 303))
    drawn = jax.random.randint(first_key, (REQUESTS,), 1, PREFIX + 1)
    full_request = jax.random.randint(second_key, (), 0, REQUESTS)
    return drawn.at[full_request].set(PREFIX).astype(jnp.int32)


def shard_levels(key, extent, shards, low, largest):
    factor_of, own = 1.0, jax.random.fold_in(key, 6)
    for dim, shards_of in shards:
        steps = jnp.exp(jax.random.uniform(jax.random.fold_in(own, dim), (shards_of,), jnp.float32, low / len(shards), largest / len(shards)))
        factor_of = factor_of * jnp.repeat(steps, extent[dim] // shards_of).reshape([-1 if axis == dim else 1 for axis in range(len(extent))])
    return factor_of


def normal_values(own_key, extent, width, limit, cuts=(), kind=jnp.bfloat16):
    values = jax.random.normal(own_key, extent, jnp.float32) * width
    if len(cuts) > 0:
        values = shard_levels(own_key, extent, cuts, -0.22, 0.18) * values
    return jnp.clip(values, min=-limit, max=limit).astype(kind)


def setup_inputs(seed: int = 0) -> dict:
    arg_keys = jax.random.split(jax.random.key(seed), 12)
    hidden_rows = normal_values(arg_keys[0], (SPAN, REQUESTS, D), 1.0, 6.0, ((0, 4), (1, 8)))
    norm_gain = jnp.clip(1.0 + 0.18 * jax.random.normal(arg_keys[1], (D,), jnp.float32), 0.1, 1.9)
    w_query = normal_values(arg_keys[2], (D, HEADS * HD), D ** -0.5, 0.0625, ((1, 4),))
    w_key = normal_values(arg_keys[3], (D, KVH * HD), D ** -0.5, 0.0625, ((1, 4),))
    w_value = normal_values(arg_keys[4], (D, KVH * HD), D ** -0.5, 0.0625, ((1, 4),))
    w_out = normal_values(arg_keys[5], (HEADS * HD, D), (HEADS * HD // 256) ** -0.5, 1.5, ((0, 4),))
    cache_keys = normal_values(arg_keys[6], (REQUESTS, PREFIX, KVH * HD), 1.0, 6.0, ((0, 8), (2, 4)))
    cache_values = normal_values(arg_keys[7], (REQUESTS, PREFIX, KVH * HD), 1.0, 6.0, ((0, 8), (2, 4)))
    slot_of_request = draw_slot_of_request(jax.random.fold_in(arg_keys[11], 71), 0)
    span_length = draw_span_length(jax.random.fold_in(arg_keys[11], 71), 0)
    prefix_length = draw_prefix_length(jax.random.fold_in(arg_keys[11], 71), 0)
    return dict(hidden_rows=hidden_rows, norm_gain=norm_gain, w_query=w_query, w_key=w_key, w_value=w_value, w_out=w_out, cache_keys=cache_keys, cache_values=cache_values, slot_of_request=slot_of_request, span_length=span_length, prefix_length=prefix_length)


rope_base = 500000.0
norm_eps = 1e-05
masked = -1e+30

def rotate(values, position):
    head_width = values.shape[-1]
    half_width = head_width // 2
    frequency = rope_base ** (-(jnp.arange(half_width, dtype=jnp.float32) * 2.0 / head_width))
    angles = position[..., None, None] * frequency
    cosine = jnp.cos(angles)
    sine_part = jnp.sin(angles)
    front_half = values[..., :half_width]
    back_half = values[..., half_width:]
    return jnp.concatenate([front_half * cosine - back_half * sine_part, back_half * cosine + front_half * sine_part], axis=-1)

def attend_one(inputs, cache_keys, cache_values):
    one_query, keys_new, values_new, slot_index, prefix_now, length_now = inputs
    span_rows = one_query.shape[0]
    groups = HEADS // KVH
    score_scale = HD ** (-0.5)
    keys_old = lax.dynamic_index_in_dim(cache_keys, slot_index.astype(jnp.int32), 0, keepdims=False)
    values_old = lax.dynamic_index_in_dim(cache_values, slot_index.astype(jnp.int32), 0, keepdims=False)
    grouped = one_query.reshape(span_rows, KVH, groups, HD).astype(jnp.float32)
    old_keys = keys_old.reshape(PREFIX, KVH, HD).astype(jnp.float32)
    old_values = values_old.reshape(PREFIX, KVH, HD).astype(jnp.float32)
    score_old = jnp.einsum('cgmd,pgd->gmcp', grouped, old_keys) * score_scale
    score_new = jnp.einsum('cgmd,jgd->gmcj', grouped, keys_new.astype(jnp.float32)) * score_scale
    keep_old = jnp.arange(PREFIX, dtype=jnp.int32) < prefix_now
    row_index = jnp.arange(span_rows, dtype=jnp.int32)
    keep_new = (row_index[None, :] < length_now) & (row_index[None, :] <= row_index[:, None])
    score_old = jnp.where(keep_old, score_old, masked)
    score_new = jnp.where(keep_new, score_new, masked)
    exp_old = jnp.exp(score_old)
    exp_new = jnp.exp(score_new)
    denominator = lax.optimization_barrier(jnp.sum(exp_old, axis=-1, keepdims=True)) + lax.optimization_barrier(jnp.sum(exp_new, axis=-1, keepdims=True))
    weight_old = (exp_old / denominator).astype(jnp.bfloat16).astype(jnp.float32)
    weight_new = (exp_new / denominator).astype(jnp.bfloat16).astype(jnp.float32)
    mixed = jnp.einsum('gmcp,pgd->cgmd', weight_old, old_values)
    mixed = mixed + jnp.einsum('gmcj,jgd->cgmd', weight_new, values_new.astype(jnp.float32))
    return mixed.astype(jnp.bfloat16).reshape(span_rows, HEADS * HD)

def reference(hidden_rows, norm_gain, w_query, w_key, w_value, w_out, cache_keys, cache_values, slot_of_request, span_length, prefix_length):
    floats = hidden_rows.astype(jnp.float32)
    normed = (floats * lax.rsqrt(lax.optimization_barrier(jnp.mean(floats * floats, axis=-1, keepdims=True)) + norm_eps) * norm_gain).astype(jnp.bfloat16)
    flat_rows = normed.reshape(SPAN * REQUESTS, D)
    positions = (prefix_length[None, :] + jnp.arange(SPAN, dtype=jnp.int32)[:, None]).astype(jnp.float32)
    queries = jnp.dot(flat_rows, w_query, preferred_element_type=jnp.float32).reshape(SPAN, REQUESTS, HEADS, HD)
    queries = rotate(queries, positions).astype(jnp.bfloat16)
    keys_new = jnp.dot(flat_rows, w_key, preferred_element_type=jnp.float32).reshape(SPAN, REQUESTS, KVH, HD)
    keys_new = rotate(keys_new, positions).astype(jnp.bfloat16)
    values_new = jnp.dot(flat_rows, w_value, preferred_element_type=jnp.float32).astype(jnp.bfloat16).reshape(SPAN, REQUESTS, KVH, HD)
    inputs = (jnp.transpose(queries, (1, 0, 2, 3)), jnp.transpose(keys_new, (1, 0, 2, 3)), jnp.transpose(values_new, (1, 0, 2, 3)), slot_of_request, prefix_length, span_length)
    heads_out = lax.map(lambda one_input: attend_one(one_input, cache_keys, cache_values), inputs)
    heads_out = jnp.transpose(heads_out, (1, 0, 2)).reshape(SPAN * REQUESTS, HEADS * HD)
    result = jnp.dot(heads_out, w_out, preferred_element_type=jnp.float32)
    return result.astype(jnp.bfloat16).reshape(SPAN, REQUESTS, D)
```

```python
import functools

import jax
import jax.numpy as jnp
from jax import lax
from jax.experimental import pallas as pl
from jax.experimental.pallas import tpu as pltpu
from jax.sharding import PartitionSpec as P

HD = 128
rope_base = 500000.0
norm_eps = 1e-05
masked = -1e30


def normalize(rows, norm_gain):
    floats = rows.astype(jnp.float32)
    return (
        floats * lax.rsqrt(jnp.mean(floats * floats, axis=-1, keepdims=True) + norm_eps) * norm_gain
    ).astype(jnp.bfloat16)


def rope_tables(first_position, span):
    half = HD // 2
    frequency = rope_base ** (-(jnp.arange(half, dtype=jnp.float32) * 2.0 / HD))
    positions = (first_position + jnp.arange(span, dtype=jnp.int32)).astype(jnp.float32)
    angles = positions[:, None] * frequency
    cosine = jnp.cos(angles)
    sine = jnp.sin(angles)
    return lax.optimization_barrier(
        (jnp.concatenate([cosine, cosine], axis=1), jnp.concatenate([-sine, sine], axis=1))
    )


def project_kernel(
    tiles, x_hbm, wq_hbm, wk_hbm, wv_hbm, cos_ref, sin_ref, out_ref, x_ref, w_ref, x_sem, w_sem
):
    sources = (wq_hbm, wk_hbm, wv_hbm)
    x_copy = pltpu.make_async_copy(x_hbm, x_ref, x_sem)
    copies = []
    offset = 0
    for index, (which, column, width, _) in enumerate(tiles):
        copies.append(
            pltpu.make_async_copy(
                sources[which].at[:, pl.ds(column, width)],
                w_ref.at[:, pl.ds(offset, width)],
                w_sem.at[index],
            )
        )
        offset += width
    copies[0].start()
    x_copy.start()
    for copy in copies[1:]:
        copy.start()
    x_copy.wait()
    offset = 0
    for copy, (_, _, width, rotated) in zip(copies, tiles):
        copy.wait()
        product = jnp.dot(
            x_ref[...], w_ref[:, offset : offset + width], preferred_element_type=jnp.float32
        )
        for head in range(width // HD):
            part = product[:, head * HD : (head + 1) * HD]
            if rotated:
                part = part * cos_ref[...] + pltpu.roll(part, HD // 2, 1) * sin_ref[...]
            out_ref[:, offset + head * HD : offset + (head + 1) * HD] = part.astype(out_ref.dtype)
        offset += width


def project(rows, w_query, w_key, w_value, tables):
    span, features = rows.shape
    q_width, kv_width = w_query.shape[1], w_key.shape[1]
    tiles = []
    for which, total, rotated in ((0, q_width, True), (1, kv_width, True), (2, kv_width, False)):
        step = min(256, total)
        tiles += [(which, column, step, rotated) for column in range(0, total, step)]
    width = q_width + 2 * kv_width
    anywhere = pl.BlockSpec(memory_space=pl.ANY)
    here = pl.BlockSpec(memory_space=pltpu.VMEM)
    return pl.pallas_call(
        functools.partial(project_kernel, tuple(tiles)),
        out_shape=jax.ShapeDtypeStruct((span, width), jnp.bfloat16),
        in_specs=[anywhere] * 4 + [here] * 2,
        out_specs=here,
        scratch_shapes=[
            pltpu.VMEM((span, features), jnp.bfloat16),
            pltpu.VMEM((features, width), jnp.bfloat16),
            pltpu.SemaphoreType.DMA,
            pltpu.SemaphoreType.DMA((len(tiles),)),
        ],
        compiler_params=pltpu.CompilerParams(vmem_limit_bytes=44 << 20),
        cost_estimate=pl.CostEstimate(
            flops=2 * span * features * width,
            bytes_accessed=2 * features * (width + span),
            transcendentals=0,
        ),
        name="project_rope",
    )(rows, w_query, w_key, w_value, *tables)


def attend_kernel(
    groups, block, facts, q_ref, kn_ref, vn_ref, kc_ref, vc_ref, out_ref, m_ref, acc_ref, ve_ref
):
    span = q_ref.shape[0]
    prefix = facts[1]
    length = facts[2]
    factor = (HD**-0.5) * 1.4426950408889634
    contract = (((1,), (1,)), ((), ()))
    ve_ref[:, HD:] = jnp.ones((block, HD), jnp.bfloat16)

    row = lax.broadcasted_iota(jnp.int32, (span, span), 0)
    column = lax.broadcasted_iota(jnp.int32, (span, span), 1)
    keep_new = (column <= row) & (column < length)
    ve_ref[:span, :HD] = vn_ref[...]
    for head in range(groups):
        query = q_ref[:, head * HD : (head + 1) * HD]
        scores = lax.dot_general(query, kn_ref[...], contract, preferred_element_type=jnp.float32)
        scores = jnp.where(keep_new, scores * factor, masked)
        top = jnp.max(scores, axis=1, keepdims=True)
        weights = jnp.exp2(scores - top).astype(jnp.bfloat16)
        m_ref[head] = jnp.broadcast_to(top, (span, HD))
        acc_ref[head] = jnp.dot(weights, ve_ref[:span, :], preferred_element_type=jnp.float32)

    def step(index, carry):
        start = pl.multiple_of(index * block, block)
        keys = kc_ref[0, pl.ds(start, block), :]
        ve_ref[:, :HD] = vc_ref[0, pl.ds(start, block), :]
        keep = (start + lax.broadcasted_iota(jnp.int32, (1, block), 1)) < prefix
        for head in range(groups):
            query = q_ref[:, head * HD : (head + 1) * HD]
            scores = lax.dot_general(query, keys, contract, preferred_element_type=jnp.float32)
            scores = jnp.where(keep, scores * factor, masked)
            before = m_ref[head]
            top = jnp.maximum(before, jnp.max(scores, axis=1, keepdims=True))
            weights = jnp.exp2(scores - top[:, :1]).astype(jnp.bfloat16)
            shrink = jnp.exp2(before - top)
            m_ref[head] = top
            acc_ref[head] = acc_ref[head] * jnp.concatenate([shrink, shrink], axis=1) + jnp.dot(
                weights, ve_ref[...], preferred_element_type=jnp.float32
            )
        return carry

    lax.fori_loop(0, lax.div(prefix + (block - 1), block), step, 0)
    for head in range(groups):
        total = acc_ref[head]
        out_ref[:, head * HD : (head + 1) * HD] = (total[:, :HD] / total[:, HD:]).astype(
            out_ref.dtype
        )


def attend(facts, packed, cache_keys, cache_values, q_width, kv_width):
    span = packed.shape[0]
    prefix = cache_keys.shape[1]
    kv_heads = kv_width // HD
    groups = q_width // kv_width
    block = min(512, prefix)
    q_tiles = q_width // HD
    return pl.pallas_call(
        functools.partial(attend_kernel, groups, block),
        out_shape=jax.ShapeDtypeStruct((span, q_width), jnp.bfloat16),
        grid_spec=pltpu.PrefetchScalarGridSpec(
            num_scalar_prefetch=1,
            grid=(kv_heads,),
            in_specs=[
                pl.BlockSpec((span, groups * HD), lambda g, facts: (0, g)),
                pl.BlockSpec((span, HD), lambda g, facts: (0, q_tiles + g)),
                pl.BlockSpec((span, HD), lambda g, facts: (0, q_tiles + kv_heads + g)),
                pl.BlockSpec((1, prefix, HD), lambda g, facts: (facts[0], 0, g)),
                pl.BlockSpec((1, prefix, HD), lambda g, facts: (facts[0], 0, g)),
            ],
            out_specs=pl.BlockSpec((span, groups * HD), lambda g, facts: (0, g)),
            scratch_shapes=[
                pltpu.VMEM((groups, span, HD), jnp.float32),
                pltpu.VMEM((groups, span, 2 * HD), jnp.float32),
                pltpu.VMEM((max(block, span), 2 * HD), jnp.bfloat16),
            ],
        ),
        compiler_params=pltpu.CompilerParams(vmem_limit_bytes=32 << 20),
        cost_estimate=pl.CostEstimate(
            flops=4 * span * q_width * (prefix + span),
            bytes_accessed=4 * prefix * kv_width + 4 * span * q_width,
            transcendentals=span * (q_width // HD) * (prefix + span),
        ),
        name="attend_slot",
    )(facts, packed, packed, packed, cache_keys, cache_values)


def exchange(values, mask, size):
    def by(bits):
        if bits == 0:
            return lambda v: v
        pairs = [(i, i ^ bits) for i in range(size)]
        return lambda v: lax.ppermute(v, "dp", pairs)

    return lax.switch(mask, [by(bits) for bits in range(size)], values)


def local(
    hidden_rows,
    norm_gain,
    w_query,
    w_key,
    w_value,
    w_out,
    cache_keys,
    cache_values,
    slot_of_request,
    span_length,
    prefix_length,
):
    data_size = lax.axis_size("dp")
    data_index = lax.axis_index("dp")
    tensor_size = lax.axis_size("tensor")
    rows, per_device = hidden_rows.shape[0], hidden_rows.shape[1]
    span = rows * tensor_size
    q_width = w_query.shape[1]
    kv_width = w_key.shape[1]
    mine = data_index * per_device + jnp.arange(per_device, dtype=jnp.int32)
    masks = (slot_of_request[mine] // per_device) ^ data_index
    near = jnp.argmax(masks == 1).astype(jnp.int32)
    far = 1 - near
    far_mask = masks[far]
    neighbour = [(i, i ^ 1) for i in range(data_size)]

    def guest(mask):
        candidates = (data_index ^ mask) * per_device + jnp.arange(per_device, dtype=jnp.int32)
        slots = slot_of_request[candidates]
        which = jnp.argmax(slots // per_device == data_index).astype(jnp.int32)
        request = candidates[which]
        return jnp.stack(
            [slots[which] % per_device, prefix_length[request], span_length[request]]
        ).astype(jnp.int32)

    def heads_of(which, normed, facts, there):
        tables = rope_tables(prefix_length[data_index * per_device + which], span)
        packed = there(project(normed, w_query, w_key, w_value, tables))
        return there(attend(facts, packed, cache_keys, cache_values, q_width, kv_width))

    def out_part(heads):
        partial = jnp.dot(heads, w_out, preferred_element_type=jnp.float32).astype(jnp.bfloat16)
        return lax.psum_scatter(partial, "tensor", scatter_dimension=0, tiled=True)

    normed_far = normalize(lax.dynamic_index_in_dim(hidden_rows, far, 1, False), norm_gain)
    all_far = lax.all_gather(normed_far, "tensor", axis=0, tiled=True)
    normed_near = normalize(lax.dynamic_index_in_dim(hidden_rows, near, 1, False), norm_gain)
    all_near = lax.all_gather(normed_near, "tensor", axis=0, tiled=True)
    heads_far = heads_of(
        far, all_far, guest(far_mask), lambda v: exchange(v, far_mask, data_size)
    )
    out_far = out_part(heads_far)
    heads_near = heads_of(
        near,
        all_near,
        guest(jnp.int32(1)),
        lambda v: lax.ppermute(v, "dp", neighbour),
    )
    out_near = out_part(heads_near)
    swap = far == 1
    return jnp.stack(
        [jnp.where(swap, out_near, out_far), jnp.where(swap, out_far, out_near)], axis=1
    )


def solution(mesh):
    placed = (
        P("tensor", "dp", None),
        P(),
        P(None, "tensor"),
        P(None, "tensor"),
        P(None, "tensor"),
        P("tensor", None),
        P("dp", None, "tensor"),
        P("dp", None, "tensor"),
        P(),
        P(),
        P(),
    )
    return jax.shard_map(
        local, mesh=mesh, in_specs=placed, out_specs=P("tensor", "dp", None), check_vma=False
    )
```

```python
import functools

import jax
import jax.numpy as jnp
from jax import lax
from jax.experimental import pallas as pl
from jax.experimental.pallas import tpu as pltpu
from jax.sharding import PartitionSpec as P

HD = 128
rope_base = 500000.0
norm_eps = 1e-05
masked = -1e30


def normalize(rows, norm_gain):
    floats = rows.astype(jnp.float32)
    return (
        floats * lax.rsqrt(jnp.mean(floats * floats, axis=-1, keepdims=True) + norm_eps) * norm_gain
    ).astype(jnp.bfloat16)


def rope_tables(first_position, span):
    half = HD // 2
    frequency = rope_base ** (-(jnp.arange(half, dtype=jnp.float32) * 2.0 / HD))
    positions = (first_position + jnp.arange(span, dtype=jnp.int32)).astype(jnp.float32)
    angles = positions[:, None] * frequency
    cosine = jnp.cos(angles)
    sine = jnp.sin(angles)
    return lax.optimization_barrier(
        (jnp.concatenate([cosine, cosine], axis=1), jnp.concatenate([-sine, sine], axis=1))
    )


def project_kernel(chunk, kv_heads, groups, x_hbm, wq_hbm, wk_hbm, wv_hbm, cos_ref, sin_ref, *rest):
    outs = rest[:kv_heads]
    x_ref, wq_ref, wk_ref, wv_ref, acc_ref, sems = rest[kv_heads:]
    features = wq_hbm.shape[0]
    steps = features // chunk

    def copies(index):
        piece = pl.ds(pl.multiple_of(index * chunk, chunk), chunk)
        return [pltpu.make_async_copy(x_hbm.at[:, piece], x_ref.at[:, piece], sems.at[0, index])] + [
            pltpu.make_async_copy(source.at[piece, :], target.at[piece, :], sems.at[1 + n, index])
            for n, (source, target) in enumerate(
                ((wq_hbm, wq_ref), (wk_hbm, wk_ref), (wv_hbm, wv_ref))
            )
        ]

    def begin(index, carry):
        for copy in copies(index):
            copy.start()
        return carry

    lax.fori_loop(0, steps, begin, 0)
    acc_ref[...] = jnp.zeros_like(acc_ref)

    def step(index, carry):
        for copy in copies(index):
            copy.wait()
        piece = pl.ds(pl.multiple_of(index * chunk, chunk), chunk)
        rows = x_ref[:, piece]
        offset = 0
        for weights in (wq_ref, wk_ref, wv_ref):
            width = weights.shape[1]
            tile = min(256, width)
            for column in range(0, width, tile):
                acc_ref[:, offset + column : offset + column + tile] += jnp.dot(
                    rows,
                    weights[piece, column : column + tile],
                    preferred_element_type=jnp.float32,
                )
            offset += width
        return carry

    lax.fori_loop(0, steps, step, 0)
    q_heads = kv_heads * groups
    for g in range(kv_heads):
        places = [g * groups + m for m in range(groups)] + [q_heads + g, q_heads + kv_heads + g]
        for slot, place in enumerate(places):
            part = acc_ref[:, place * HD : (place + 1) * HD]
            if slot <= groups:
                part = part * cos_ref[...] + pltpu.roll(part, HD // 2, 1) * sin_ref[...]
            outs[g][:, slot * HD : (slot + 1) * HD] = part.astype(jnp.bfloat16)


def project(rows, w_query, w_key, w_value, tables):
    span, features = rows.shape
    q_width, kv_width = w_query.shape[1], w_key.shape[1]
    kv_heads, groups = kv_width // HD, q_width // kv_width
    chunk = min(1024, features)
    width = q_width + 2 * kv_width
    far_memory = pl.BlockSpec(memory_space=pltpu.HBM)
    here = pl.BlockSpec(memory_space=pltpu.VMEM)
    return pl.pallas_call(
        functools.partial(project_kernel, chunk, kv_heads, groups),
        out_shape=[jax.ShapeDtypeStruct((span, (groups + 2) * HD), jnp.bfloat16)] * kv_heads,
        in_specs=[far_memory] * 4 + [here] * 2,
        out_specs=[here] * kv_heads,
        scratch_shapes=[
            pltpu.VMEM((span, features), jnp.bfloat16),
            pltpu.VMEM((features, q_width), jnp.bfloat16),
            pltpu.VMEM((features, kv_width), jnp.bfloat16),
            pltpu.VMEM((features, kv_width), jnp.bfloat16),
            pltpu.VMEM((span, width), jnp.float32),
            pltpu.SemaphoreType.DMA((4, features // chunk)),
        ],
        compiler_params=pltpu.CompilerParams(vmem_limit_bytes=44 << 20),
        cost_estimate=pl.CostEstimate(
            flops=2 * span * features * width,
            bytes_accessed=2 * features * (width + span),
            transcendentals=0,
        ),
        name="project_rope",
    )(rows, w_query, w_key, w_value, *tables)


def attend_kernel(
    groups, block, facts, packed_ref, kc_ref, vc_ref, out_ref, m_ref, acc_ref, ve_ref
):
    span = packed_ref.shape[0]
    q_ref = packed_ref
    prefix = facts[1]
    length = facts[2]
    factor = (HD**-0.5) * 1.4426950408889634
    contract = (((1,), (1,)), ((), ()))
    ve_ref[:, HD:] = jnp.ones((block, HD), jnp.bfloat16)

    row = lax.broadcasted_iota(jnp.int32, (span, span), 0)
    column = lax.broadcasted_iota(jnp.int32, (span, span), 1)
    keep_new = (column <= row) & (column < length)
    ve_ref[:span, :HD] = packed_ref[:, (groups + 1) * HD :]
    for head in range(groups):
        query = q_ref[:, head * HD : (head + 1) * HD]
        scores = lax.dot_general(query, packed_ref[:, groups * HD : (groups + 1) * HD], contract, preferred_element_type=jnp.float32)
        scores = jnp.where(keep_new, scores * factor, masked)
        top = jnp.max(scores, axis=1, keepdims=True)
        weights = jnp.exp2(scores - top).astype(jnp.bfloat16)
        m_ref[head] = jnp.broadcast_to(top, (span, HD))
        acc_ref[head] = jnp.dot(weights, ve_ref[:span, :], preferred_element_type=jnp.float32)

    def step(index, carry):
        start = pl.multiple_of(index * block, block)
        keys = kc_ref[0, pl.ds(start, block), :]
        ve_ref[:, :HD] = vc_ref[0, pl.ds(start, block), :]
        keep = (start + lax.broadcasted_iota(jnp.int32, (1, block), 1)) < prefix
        for head in range(groups):
            query = q_ref[:, head * HD : (head + 1) * HD]
            scores = lax.dot_general(query, keys, contract, preferred_element_type=jnp.float32)
            scores = jnp.where(keep, scores * factor, masked)
            before = m_ref[head]
            top = jnp.maximum(before, jnp.max(scores, axis=1, keepdims=True))
            weights = jnp.exp2(scores - top[:, :1]).astype(jnp.bfloat16)
            shrink = jnp.exp2(before - top)
            m_ref[head] = top
            acc_ref[head] = acc_ref[head] * jnp.concatenate([shrink, shrink], axis=1) + jnp.dot(
                weights, ve_ref[...], preferred_element_type=jnp.float32
            )
        return carry

    lax.fori_loop(0, lax.div(prefix + (block - 1), block), step, 0)
    for head in range(groups):
        total = acc_ref[head]
        out_ref[:, head * HD : (head + 1) * HD] = (total[:, :HD] / total[:, HD:]).astype(
            out_ref.dtype
        )


def attend(facts, packed, cache_keys, cache_values, kv_head):
    span, width = packed.shape
    prefix = cache_keys.shape[1]
    groups = width // HD - 2
    block = min(512, prefix)
    return pl.pallas_call(
        functools.partial(attend_kernel, groups, block),
        out_shape=jax.ShapeDtypeStruct((span, groups * HD), jnp.bfloat16),
        grid_spec=pltpu.PrefetchScalarGridSpec(
            num_scalar_prefetch=1,
            grid=(1,),
            in_specs=[
                pl.BlockSpec((span, width), lambda i, facts: (0, 0)),
                pl.BlockSpec((1, prefix, HD), lambda i, facts: (facts[0], 0, kv_head)),
                pl.BlockSpec((1, prefix, HD), lambda i, facts: (facts[0], 0, kv_head)),
            ],
            out_specs=pl.BlockSpec((span, groups * HD), lambda i, facts: (0, 0)),
            scratch_shapes=[
                pltpu.VMEM((groups, span, HD), jnp.float32),
                pltpu.VMEM((groups, span, 2 * HD), jnp.float32),
                pltpu.VMEM((max(block, span), 2 * HD), jnp.bfloat16),
            ],
        ),
        compiler_params=pltpu.CompilerParams(vmem_limit_bytes=32 << 20),
        cost_estimate=pl.CostEstimate(
            flops=4 * span * groups * HD * (prefix + span),
            bytes_accessed=4 * prefix * HD + 4 * span * groups * HD,
            transcendentals=span * groups * (prefix + span),
        ),
        name="attend_head_group",
    )(facts, packed, cache_keys, cache_values)


def out_kernel(pieces, *refs):
    heads, w_ref, out_ref = refs[:pieces], refs[pieces], refs[-1]
    depth = heads[0].shape[1]
    total = None
    for index, piece in enumerate(heads):
        term = jnp.dot(
            piece[...],
            w_ref[index * depth : (index + 1) * depth, :],
            preferred_element_type=jnp.float32,
        )
        total = term if total is None else total + term
    out_ref[...] = total.astype(out_ref.dtype)


def out_columns(heads, w_out, first, columns):
    span, depth = heads[0].shape
    inputs = w_out.shape[0]
    tile = min(1024, columns)
    whole = pl.BlockSpec((span, depth), lambda i: (0, 0))
    return pl.pallas_call(
        functools.partial(out_kernel, len(heads)),
        out_shape=jax.ShapeDtypeStruct((span, columns), jnp.bfloat16),
        grid=(columns // tile,),
        in_specs=[whole] * len(heads)
        + [pl.BlockSpec((inputs, tile), lambda i: (0, first // tile + i))],
        out_specs=pl.BlockSpec((span, tile), lambda i: (0, i)),
        compiler_params=pltpu.CompilerParams(vmem_limit_bytes=32 << 20),
        cost_estimate=pl.CostEstimate(
            flops=2 * span * inputs * columns,
            bytes_accessed=2 * (inputs + span) * columns,
            transcendentals=0,
        ),
        name="out_columns",
    )(*heads, w_out)


def out_lent_kernel(pieces, order, me_ref, *refs):
    heads = refs[:pieces]
    lent_ref, w_ref, near_ref, far_ref, out_ref, sorted_ref = refs[pieces:]
    width = lent_ref.shape[1] // len(order)

    @pl.when(pl.program_id(0) == 0)
    def _():
        for place, bits in enumerate(order):
            start = pl.multiple_of((me_ref[0] ^ bits) * width, width)
            sorted_ref[:, place * width : (place + 1) * width] = lent_ref[:, pl.ds(start, width)]

    depth = heads[0].shape[1]
    half = near_ref.shape[0]
    total = jnp.dot(sorted_ref[:, :half], near_ref[...], preferred_element_type=jnp.float32)
    total += jnp.dot(sorted_ref[:, half:], far_ref[...], preferred_element_type=jnp.float32)
    for index, piece in enumerate(heads):
        total += jnp.dot(
            piece[...],
            w_ref[index * depth : (index + 1) * depth, :],
            preferred_element_type=jnp.float32,
        )
    out_ref[...] = total.astype(out_ref.dtype)


def out_columns_lent(heads, lent_heads, w_out, lent_near, lent_far, order, me):
    span, depth = heads[0].shape
    inputs = w_out.shape[0]
    columns = lent_near.shape[1]
    tile = min(1024, columns)
    half = lent_near.shape[0]
    return pl.pallas_call(
        functools.partial(out_lent_kernel, len(heads), order),
        out_shape=jax.ShapeDtypeStruct((span, columns), jnp.bfloat16),
        grid_spec=pltpu.PrefetchScalarGridSpec(
            num_scalar_prefetch=1,
            grid=(columns // tile,),
            in_specs=[pl.BlockSpec((span, depth), lambda i, me: (0, 0))] * len(heads)
            + [
                pl.BlockSpec((span, inputs), lambda i, me: (0, 0)),
                pl.BlockSpec((inputs, tile), lambda i, me: (0, i)),
                pl.BlockSpec((half, tile), lambda i, me: (0, i)),
                pl.BlockSpec((half, tile), lambda i, me: (0, i)),
            ],
            out_specs=pl.BlockSpec((span, tile), lambda i, me: (0, i)),
            scratch_shapes=[pltpu.VMEM((span, inputs), jnp.bfloat16)],
        ),
        compiler_params=pltpu.CompilerParams(vmem_limit_bytes=32 << 20),
        cost_estimate=pl.CostEstimate(
            flops=4 * span * inputs * columns,
            bytes_accessed=2 * (2 * inputs + span) * columns,
            transcendentals=0,
        ),
        name="out_columns_lent",
    )(me, *heads, lent_heads, w_out, lent_near, lent_far)


def add_rows(partial, index, rows, *received):
    mine = lax.dynamic_slice_in_dim(partial, index * rows, rows, 0)
    if not received:
        return mine
    total = mine.astype(jnp.float32)
    for other in received:
        total = total + other.astype(jnp.float32)
    return total.astype(jnp.bfloat16)


def line_sum(partial, place, size):
    rows = partial.shape[0] // size
    last = size - 1
    first = lax.ppermute(
        add_rows(partial, jnp.where(place == 0, last, 0), rows),
        "tensor",
        [(0, 1), (last, last - 1)],
    )
    up = down = first
    for step in range(2, size):
        sent_up = add_rows(partial, jnp.clip(place + size - step, 0, last), rows, up)
        sent_down = add_rows(partial, jnp.clip(place - size + step, 0, last), rows, down)
        up = lax.ppermute(sent_up, "tensor", [(a, a + 1) for a in range(step)])
        down = lax.ppermute(sent_down, "tensor", [(a, a - 1) for a in range(size - step, size)])
    return add_rows(partial, place, rows, up, down)


def lent_sum(partial, place):
    rows = partial.shape[0] // 4
    low = place <= 1
    middle = [(1, 2), (2, 1)]
    outer = lax.ppermute(add_rows(partial, jnp.where(low, 3, 0), rows), "tensor", middle)
    inner = lax.ppermute(add_rows(partial, jnp.where(low, 2, 1), rows), "tensor", middle)
    ends = lax.ppermute(
        add_rows(partial, jnp.where(low, 0, 3), rows, outer), "tensor", [(2, 3), (1, 0)]
    )
    return add_rows(partial, place, rows, inner, ends)


def lend_weights(w_out, columns, data_index, data_size):
    def by(bits):
        return [(i, i ^ bits) for i in range(data_size)]

    rows = w_out.shape[0] // data_size
    own = lax.dynamic_slice(w_out, (data_index * rows, 0), (rows, columns))
    own = lax.ppermute(own, "tensor", [(0, 1), (3, 2)])
    by_two = lax.ppermute(own, "dp", by(2))
    by_four = lax.ppermute(own, "dp", by(4))
    by_six_low = lax.ppermute(by_two[: rows // 2], "dp", by(4))
    by_six_high = lax.ppermute(by_four[rows // 2 :], "dp", by(2))
    near = jnp.concatenate([own, by_two, by_four, by_six_low, by_six_high], axis=0)
    return near, lax.ppermute(near, "dp", by(1))


def local(
    hidden_rows,
    norm_gain,
    w_query,
    w_key,
    w_value,
    w_out,
    cache_keys,
    cache_values,
    slot_of_request,
    span_length,
    prefix_length,
):
    data_size = lax.axis_size("dp")
    data_index = lax.axis_index("dp")
    tensor_size = lax.axis_size("tensor")
    place = lax.axis_index("tensor")
    rows, per_device, model = hidden_rows.shape
    span = rows * tensor_size
    q_width = w_query.shape[1]
    kv_width = w_key.shape[1]
    kv_heads = kv_width // HD
    first_slot = lax.dynamic_index_in_dim(slot_of_request, data_index * per_device, 0, False)
    first_mask = (first_slot // per_device) ^ data_index
    far = jnp.where(first_mask == 1, 1, 0).astype(jnp.int32)
    near = 1 - far
    neighbour = [(i, i ^ 1) for i in range(data_size)]
    lends = tensor_size == 4 and data_size == 8
    lent_columns = model // 2

    normed_far = normalize(lax.dynamic_index_in_dim(hidden_rows, far, 1, False), norm_gain)
    hidden_rows, normed_far = lax.optimization_barrier((hidden_rows, normed_far))
    all_far = lax.all_gather(normed_far, "tensor", axis=0, tiled=True)
    normed_near = normalize(lax.dynamic_index_in_dim(hidden_rows, near, 1, False), norm_gain)
    all_near = lax.all_gather(normed_near, "tensor", axis=0, tiled=True)

    my_slots = lax.dynamic_slice_in_dim(slot_of_request, data_index * per_device, per_device)
    far_mask = (lax.dynamic_index_in_dim(my_slots, far, 0, False) // per_device) ^ data_index

    def guest(mask):
        host = (data_index ^ mask) * per_device
        slots = lax.dynamic_slice_in_dim(slot_of_request, host, per_device)
        which = jnp.where(slots[0] // per_device == data_index, 0, 1)
        slot = jnp.where(which == 0, slots[0], slots[1])
        return jnp.stack(
            [slot % per_device, prefix_length[host + which], span_length[host + which]]
        ).astype(jnp.int32)

    def packed_of(which, normed):
        tables = rope_tables(prefix_length[data_index * per_device + which], span)
        return project(normed, w_query, w_key, w_value, tables)

    def heads_by(bits, facts):
        def there(values):
            if bits == 0:
                return values
            return lax.ppermute(values, "dp", [(i, i ^ bits) for i in range(data_size)])

        def run(*packed):
            moved = [there(piece) for piece in packed]
            return tuple(
                there(attend(facts, piece, cache_keys, cache_values, g))
                for g, piece in enumerate(moved)
            )

        return run

    if lends:
        lent_near, lent_far = lend_weights(w_out, lent_columns, data_index, data_size)
        order = (0, 2, 4, 6, 1, 3, 5, 7)
        in_place = (jnp.arange(span, dtype=jnp.int32) // rows == place)[:, None]

    def out_parts(heads):
        if not lends:
            partial = out_columns(heads, w_out, 0, model)
            return [lax.psum_scatter(partial, "tensor", scatter_dimension=0, tiled=True)]
        lent_heads = jnp.where(in_place, jnp.bfloat16(0), jnp.concatenate(heads, axis=1))
        lent_heads = lax.ppermute(lent_heads, "tensor", [(0, 1), (3, 2)])
        plain = out_columns(heads, w_out, lent_columns, model - lent_columns)
        summed_plain = line_sum(plain, place, tensor_size)
        lent = out_columns_lent(
            heads, lent_heads, w_out, lent_near, lent_far, order, data_index[None].astype(jnp.int32)
        )
        return [lent_sum(lent, place), summed_plain]

    far_facts = guest(far_mask)
    heads_far = lax.switch(
        far_mask,
        [heads_by(bits, far_facts) for bits in range(data_size)],
        *packed_of(far, all_far),
    )
    out_far = out_parts(heads_far)
    heads_near = heads_by(1, guest(jnp.int32(1)))(*packed_of(near, all_near))
    out_near = out_parts(heads_near)
    swap = far == 1
    pairs = list(zip(out_far, out_near))
    first = jnp.concatenate([jnp.where(swap, b, a) for a, b in pairs], axis=1)
    second = jnp.concatenate([jnp.where(swap, a, b) for a, b in pairs], axis=1)
    return jnp.stack([first, second], axis=1)


def solution(mesh):
    placed = (
        P("tensor", "dp", None),
        P(),
        P(None, "tensor"),
        P(None, "tensor"),
        P(None, "tensor"),
        P("tensor", None),
        P("dp", None, "tensor"),
        P("dp", None, "tensor"),
        P(),
        P(),
        P(),
    )
    return jax.shard_map(
        local, mesh=mesh, in_specs=placed, out_specs=P("tensor", "dp", None), check_vma=False
    )
```

```python
import functools

import jax
import jax.numpy as jnp
from jax import lax
from jax.experimental import pallas as pl
from jax.experimental.pallas import tpu as pltpu
from jax.sharding import PartitionSpec as P

HD = 128
rope_base = 500000.0
norm_eps = 1e-05
masked = -1e30


def normalize(rows, norm_gain):
    floats = rows.astype(jnp.float32)
    return (
        floats * lax.rsqrt(jnp.mean(floats * floats, axis=-1, keepdims=True) + norm_eps) * norm_gain
    ).astype(jnp.bfloat16)


def rope_tables(first_position, span):
    half = HD // 2
    frequency = rope_base ** (-(jnp.arange(half, dtype=jnp.float32) * 2.0 / HD))
    positions = (first_position + jnp.arange(span, dtype=jnp.int32)).astype(jnp.float32)
    angles = positions[:, None] * frequency
    cosine = jnp.cos(angles)
    sine = jnp.sin(angles)
    return lax.optimization_barrier(
        (jnp.concatenate([cosine, cosine], axis=1), jnp.concatenate([-sine, sine], axis=1))
    )


def facts_kernel(per_device, slots_ref, spans_ref, prefixes_ref, out_ref):
    me = lax.axis_index("dp")
    base = me * per_device
    far = jnp.where(lax.div(slots_ref[base], per_device) ^ me == 1, 1, 0)
    far_mask = lax.div(slots_ref[base + far], per_device) ^ me
    out_ref[0] = far
    out_ref[1] = far_mask
    for start, mask in ((2, 1), (5, far_mask)):
        host = (me ^ mask) * per_device
        which = jnp.where(lax.div(slots_ref[host], per_device) == me, 0, 1)
        out_ref[start] = lax.rem(slots_ref[host + which], per_device)
        out_ref[start + 1] = prefixes_ref[host + which]
        out_ref[start + 2] = spans_ref[host + which]
    out_ref[8] = prefixes_ref[base + 1 - far]


def find_facts(slots, spans, prefixes, per_device):
    scalars = pl.BlockSpec(memory_space=pltpu.SMEM)
    return pl.pallas_call(
        functools.partial(facts_kernel, per_device),
        out_shape=jax.ShapeDtypeStruct((9,), jnp.int32),
        in_specs=[scalars] * 3,
        out_specs=scalars,
        name="find_facts",
    )(slots, spans, prefixes)


def project_kernel(chunk, kv_heads, groups, halves, sources, token_ref, *refs):
    count = halves * sources
    pieces = [refs[h * sources : (h + 1) * sources] for h in range(halves)]
    wq_hbm, wk_hbm, wv_hbm, cos_ref, sin_ref = refs[count : count + 5]
    outs = refs[count + 5 : count + 5 + kv_heads]
    done_ref, x_ref, wq_ref, wk_ref, wv_ref, acc_ref, x_sems, sems = refs[count + 5 + kv_heads :]
    done_ref[0] = 0
    features = wq_hbm.shape[0]
    steps = features // chunk
    rows, width = pieces[0][0].shape
    place = lax.axis_index("tensor")

    def row_copies(half, act):
        columns = pl.ds(half * width, width)

        def copy(n, first):
            start = pl.multiple_of(first * rows, rows)
            act(
                pltpu.make_async_copy(
                    pieces[half][n], x_ref.at[pl.ds(start, pieces[half][n].shape[0]), columns],
                    x_sems.at[half, n],
                )
            )

        if sources == 1:
            copy(0, 0)
            return
        copy(0, place)
        for n, first, held in (
            (1, place - 1, place >= 1),
            (2, place + 1, place <= 2),
            (3, place - 2, place >= 2),
            (4, place + 2, place <= 1),
            (5, 3 - place, (place == 0) | (place == 3)),
        ):
            pl.when(held)(functools.partial(copy, n, first))

    def copies(index):
        piece = pl.ds(pl.multiple_of(index * chunk, chunk), chunk)
        return [
            pltpu.make_async_copy(source.at[piece, :], target.at[piece, :], sems.at[n, index])
            for n, (source, target) in enumerate(
                ((wq_hbm, wq_ref), (wk_hbm, wk_ref), (wv_hbm, wv_ref))
            )
        ]

    def begin(index, carry):
        for copy in copies(index):
            copy.start()
        return carry

    row_copies(0, lambda copy: copy.start())
    lax.fori_loop(0, 1, begin, 0)
    for half in range(1, halves):
        row_copies(half, lambda copy: copy.start())
    lax.fori_loop(1, steps, begin, 0)
    acc_ref[...] = jnp.zeros_like(acc_ref)

    def step(index, carry):
        for copy in copies(index):
            copy.wait()
        piece = pl.ds(pl.multiple_of(index * chunk, chunk), chunk)
        block = x_ref[:, piece]
        offset = 0
        for weights in (wq_ref, wk_ref, wv_ref):
            total = weights.shape[1]
            tile = min(256, total)
            for column in range(0, total, tile):
                acc_ref[:, offset + column : offset + column + tile] += jnp.dot(
                    block,
                    weights[piece, column : column + tile],
                    preferred_element_type=jnp.float32,
                )
            offset += total
        return carry

    each = steps // halves
    for half in range(halves):
        row_copies(half, lambda copy: copy.wait())
        lax.fori_loop(half * each, (half + 1) * each, step, 0)
    q_heads = kv_heads * groups
    for g in range(kv_heads):
        places = [g * groups + m for m in range(groups)] + [q_heads + g, q_heads + kv_heads + g]
        for slot, where in enumerate(places):
            part = acc_ref[:, where * HD : (where + 1) * HD]
            if slot <= groups:
                part = part * cos_ref[...] + pltpu.roll(part, HD // 2, 1) * sin_ref[...]
            outs[g][:, slot * HD : (slot + 1) * HD] = part.astype(jnp.bfloat16)


def project(pieces, w_query, w_key, w_value, tables, token):
    span = tables[0].shape[0]
    features = w_query.shape[0]
    q_width, kv_width = w_query.shape[1], w_key.shape[1]
    kv_heads, groups = kv_width // HD, q_width // kv_width
    halves, sources = len(pieces), len(pieces[0])
    chunk = min(1024, features // halves)
    width = q_width + 2 * kv_width
    far_memory = pl.BlockSpec(memory_space=pltpu.HBM)
    here = pl.BlockSpec(memory_space=pltpu.VMEM)
    return pl.pallas_call(
        functools.partial(project_kernel, chunk, kv_heads, groups, halves, sources),
        out_shape=[jax.ShapeDtypeStruct((span, (groups + 2) * HD), jnp.bfloat16)] * kv_heads
        + [jax.ShapeDtypeStruct((1,), jnp.int32)],
        in_specs=[pl.BlockSpec(memory_space=pltpu.SMEM)]
        + [far_memory] * (halves * sources + 3)
        + [here] * 2,
        out_specs=[here] * kv_heads + [pl.BlockSpec(memory_space=pltpu.SMEM)],
        scratch_shapes=[
            pltpu.VMEM((span, features), jnp.bfloat16),
            pltpu.VMEM((features, q_width), jnp.bfloat16),
            pltpu.VMEM((features, kv_width), jnp.bfloat16),
            pltpu.VMEM((features, kv_width), jnp.bfloat16),
            pltpu.VMEM((span, width), jnp.float32),
            pltpu.SemaphoreType.DMA((halves, sources)),
            pltpu.SemaphoreType.DMA((3, features // chunk)),
        ],
        compiler_params=pltpu.CompilerParams(vmem_limit_bytes=56 << 20),
        cost_estimate=pl.CostEstimate(flops=2 * span * features * width, bytes_accessed=2 * features * (width + span), transcendentals=0),
        name="project_rope",
    )(token, *[piece for half in pieces for piece in half], w_query, w_key, w_value, *tables)


def attend_kernel(
    groups, block, facts, packed_ref, kc_ref, vc_ref, out_ref, done_ref, m_ref, acc_ref, ve_ref
):
    done_ref[0] = 0
    span = packed_ref.shape[0]
    q_ref = packed_ref
    prefix = facts[1]
    length = facts[2]
    factor = (HD**-0.5) * 1.4426950408889634
    contract = (((1,), (1,)), ((), ()))
    ve_ref[:, HD:] = jnp.ones((block, HD), jnp.bfloat16)

    row = lax.broadcasted_iota(jnp.int32, (span, span), 0)
    column = lax.broadcasted_iota(jnp.int32, (span, span), 1)
    keep_new = (column <= row) & (column < length)
    ve_ref[:span, :HD] = packed_ref[:, (groups + 1) * HD :]
    for head in range(groups):
        query = q_ref[:, head * HD : (head + 1) * HD]
        scores = lax.dot_general(query, packed_ref[:, groups * HD : (groups + 1) * HD], contract, preferred_element_type=jnp.float32)
        scores = jnp.where(keep_new, scores * factor, masked)
        top = jnp.max(scores, axis=1, keepdims=True)
        weights = jnp.exp2(scores - top).astype(jnp.bfloat16)
        m_ref[head] = jnp.broadcast_to(top, (span, HD))
        acc_ref[head] = jnp.dot(weights, ve_ref[:span, :], preferred_element_type=jnp.float32)

    def step(index, carry):
        start = pl.multiple_of(index * block, block)
        keys = kc_ref[0, pl.ds(start, block), :]
        ve_ref[:, :HD] = vc_ref[0, pl.ds(start, block), :]
        keep = (start + lax.broadcasted_iota(jnp.int32, (1, block), 1)) < prefix
        for head in range(groups):
            query = q_ref[:, head * HD : (head + 1) * HD]
            scores = lax.dot_general(query, keys, contract, preferred_element_type=jnp.float32)
            scores = jnp.where(keep, scores * factor, masked)
            before = m_ref[head]
            top = jnp.maximum(before, jnp.max(scores, axis=1, keepdims=True))
            weights = jnp.exp2(scores - top[:, :1]).astype(jnp.bfloat16)
            shrink = jnp.exp2(before - top)
            m_ref[head] = top
            acc_ref[head] = acc_ref[head] * jnp.concatenate([shrink, shrink], axis=1) + jnp.dot(
                weights, ve_ref[...], preferred_element_type=jnp.float32
            )
        return carry

    lax.fori_loop(0, lax.div(prefix + (block - 1), block), step, 0)
    for head in range(groups):
        total = acc_ref[head]
        out_ref[:, head * HD : (head + 1) * HD] = (total[:, :HD] / total[:, HD:]).astype(
            out_ref.dtype
        )


def attend(facts, packed, cache_keys, cache_values, kv_head):
    span, width = packed.shape
    prefix = cache_keys.shape[1]
    groups = width // HD - 2
    block = min(1024, prefix)
    return pl.pallas_call(
        functools.partial(attend_kernel, groups, block),
        out_shape=[
            jax.ShapeDtypeStruct((span, groups * HD), jnp.bfloat16),
            jax.ShapeDtypeStruct((1,), jnp.int32),
        ],
        grid_spec=pltpu.PrefetchScalarGridSpec(
            num_scalar_prefetch=1,
            grid=(1,),
            in_specs=[
                pl.BlockSpec((span, width), lambda i, facts: (0, 0)),
                pl.BlockSpec((1, prefix, HD), lambda i, facts: (facts[0], 0, kv_head)),
                pl.BlockSpec((1, prefix, HD), lambda i, facts: (facts[0], 0, kv_head)),
            ],
            out_specs=[
                pl.BlockSpec((span, groups * HD), lambda i, facts: (0, 0)),
                pl.BlockSpec(memory_space=pltpu.SMEM),
            ],
            scratch_shapes=[
                pltpu.VMEM((groups, span, HD), jnp.float32),
                pltpu.VMEM((groups, span, 2 * HD), jnp.float32),
                pltpu.VMEM((max(block, span), 2 * HD), jnp.bfloat16),
            ],
        ),
        compiler_params=pltpu.CompilerParams(vmem_limit_bytes=56 << 20),
        cost_estimate=pl.CostEstimate(flops=1, bytes_accessed=1, transcendentals=0),
        name="attend_head_group",
    )(facts, packed, cache_keys, cache_values)


def out_kernel(pieces, earlier, parts, line, tile, *refs):
    heads, w_hbm = refs[:pieces], refs[pieces]
    refs = refs[pieces + 1 + earlier :]
    outs = refs[:parts]
    firsts = refs[parts : 2 * parts] if line else ()
    done_ref, w_ref, sems = refs[-3:]
    done_ref[0] = 0
    depth = heads[0].shape[1]
    columns = outs[0].shape[1]

    def copy(index):
        here = pl.ds(pl.multiple_of(index * tile, tile), tile)
        return pltpu.make_async_copy(w_hbm.at[:, here], w_ref.at[:, here], sems.at[index])

    def begin(index, carry):
        copy(index).start()
        return carry

    steps = columns // tile
    lax.fori_loop(0, parts * steps, begin, 0)
    if line:
        rows = firsts[0].shape[0]
        last = outs[0].shape[0] - rows
        start = pl.multiple_of(jnp.where(lax.axis_index("tensor") == 0, last, 0), rows)
    for part in range(parts):

        def step(index, carry):
            copy(index + part * steps).wait()
            there = pl.ds(pl.multiple_of((index + part * steps) * tile, tile), tile)
            here = pl.ds(pl.multiple_of(index * tile, tile), tile)
            total = None
            for place, piece in enumerate(heads):
                term = jnp.dot(
                    piece[...],
                    w_ref[place * depth : (place + 1) * depth, there],
                    preferred_element_type=jnp.float32,
                )
                total = term if total is None else total + term
            outs[part][:, here] = total.astype(outs[part].dtype)
            return carry

        lax.fori_loop(0, steps, step, 0)
        if line:
            firsts[part][...] = outs[part][pl.ds(start, rows), :]


def out_columns(heads, w_out, parts, line, earlier=()):
    span, depth = heads[0].shape
    inputs, columns = w_out.shape
    width = columns // parts
    tile = min(512, width)
    here = pl.BlockSpec(memory_space=pltpu.VMEM)
    far_memory = pl.BlockSpec(memory_space=pltpu.HBM)
    shapes = [jax.ShapeDtypeStruct((span, width), jnp.bfloat16)] * parts
    if line:
        shapes += [jax.ShapeDtypeStruct((span // 4, width), jnp.bfloat16)] * parts
    results = pl.pallas_call(
        functools.partial(out_kernel, len(heads), len(earlier), parts, line, tile),
        out_shape=shapes + [jax.ShapeDtypeStruct((1,), jnp.int32)],
        in_specs=[here] * len(heads) + [far_memory] * (1 + len(earlier)),
        out_specs=[here] * len(shapes) + [pl.BlockSpec(memory_space=pltpu.SMEM)],
        scratch_shapes=[
            pltpu.VMEM((inputs, columns), jnp.bfloat16),
            pltpu.SemaphoreType.DMA((columns // tile,)),
        ],
        compiler_params=pltpu.CompilerParams(vmem_limit_bytes=56 << 20),
        cost_estimate=pl.CostEstimate(flops=1, bytes_accessed=1, transcendentals=0),
        name="out_columns",
    )(*heads, w_out, *earlier)
    return results[:parts], results[parts:-1], results[-1]


def add_rows(partial, index, rows, *received):
    mine = lax.dynamic_slice_in_dim(partial, index * rows, rows, 0)
    if not received:
        return mine
    total = mine.astype(jnp.float32)
    for other in received:
        total = total + other.astype(jnp.float32)
    return total.astype(jnp.bfloat16)


def gather_first(own):
    up = lax.ppermute(own, "tensor", [(0, 1), (1, 2), (2, 3)])
    down = lax.ppermute(own, "tensor", [(1, 0), (2, 1), (3, 2)])
    return up, down


def gather_second(up, down):
    up_two = lax.ppermute(up, "tensor", [(1, 2), (2, 3)])
    down_two = lax.ppermute(down, "tensor", [(1, 0), (2, 1)])
    return up_two, down_two


def gather_third(up_two, down_two, place):
    held = jnp.where(place >= 2, up_two, down_two)
    return lax.ppermute(held, "tensor", [(2, 3), (1, 0)])


def sum_first(ends):
    return lax.ppermute(ends, "tensor", [(0, 1), (3, 2)])


def sum_next(partial, place, step, up, down, token):
    place = place + token[0]
    rows = partial.shape[0] // 4
    sent_up = add_rows(partial, jnp.clip(place + 4 - step, 0, 3), rows, up)
    sent_down = add_rows(partial, jnp.clip(place - 4 + step, 0, 3), rows, down)
    return (
        lax.ppermute(sent_up, "tensor", [(a, a + 1) for a in range(step)]),
        lax.ppermute(sent_down, "tensor", [(a, a - 1) for a in range(4 - step, 4)]),
    )


def local(
    hidden_rows,
    norm_gain,
    w_query,
    w_key,
    w_value,
    w_out,
    cache_keys,
    cache_values,
    slot_of_request,
    span_length,
    prefix_length,
):
    data_size = lax.axis_size("dp")
    data_index = lax.axis_index("dp")
    tensor_size = lax.axis_size("tensor")
    place = lax.axis_index("tensor")
    rows, per_device, model = hidden_rows.shape
    span = rows * tensor_size
    q_width = w_query.shape[1]
    kv_width = w_key.shape[1]
    kv_heads = kv_width // HD
    line = tensor_size == 4
    cut = model // 2

    facts = find_facts(slot_of_request, span_length, prefix_length, per_device)
    far, far_mask = facts[0], facts[1]

    def by(bits):
        if bits == 0:
            return lambda values: values
        pairs = [(i, i ^ bits) for i in range(data_size)]
        return lambda values: lax.ppermute(values, "dp", pairs)

    near_by = by(1)

    def attend_all(packed, slot_facts):
        results = [
            attend(slot_facts, piece, cache_keys, cache_values, g) for g, piece in enumerate(packed)
        ]
        return [heads for heads, _ in results], sum(token for _, token in results)

    nothing = jnp.zeros((1,), jnp.int32)
    swap = far == 1
    near_rows = jnp.where(swap, hidden_rows[:, 0, :], hidden_rows[:, 1, :])
    far_rows = jnp.where(swap, hidden_rows[:, 1, :], hidden_rows[:, 0, :])
    near_tables = rope_tables(facts[8], span)
    far_tables = rope_tables(facts[6], span)
    normed_near = normalize(near_rows, norm_gain)
    if line:

        def begin(bits):
            def run(rows, own):
                pieces = [own[:, c : c + cut] for c in (0, cut)]
                rows = by(bits)(rows)
                one = [gather_first(piece) for piece in pieces]
                two = [gather_second(*pair) for pair in one]
                three = [gather_third(*pair, place) for pair in two]
                gathered = [[p, *q, *r, t] for p, q, r, t in zip(pieces, one, two, three)]
                return gathered, normalize(rows, norm_gain)

            return run

        near_pieces, normed_far = lax.switch(
            far_mask, [begin(bits) for bits in range(data_size)], far_rows, normed_near
        )
        far_one = gather_first(normed_far)
    else:
        near_pieces = [[lax.all_gather(normed_near, "tensor", axis=0, tiled=True)]]
        far_rows = lax.switch(far_mask, [by(bits) for bits in range(data_size)], far_rows)
        normed_far = normalize(far_rows, norm_gain)
        far_pieces = [[lax.all_gather(normed_far, "tensor", axis=0, tiled=True)]]
    *packed, token = project(near_pieces, w_query, w_key, w_value, near_tables, nothing)
    if line:
        behind = token[0].astype(jnp.bfloat16)
        far_two = gather_second(*(piece + behind for piece in far_one))
    heads, token = attend_all([near_by(p) for p in packed], facts[2:5])
    if line:
        far_three = gather_third(*far_two, place + token[0])
        far_pieces = [[normed_far, *far_one, *far_two, far_three]]
    near_parts, near_ends, token = out_columns([near_by(p) for p in heads], w_out, 1, line)
    *packed, token = project(far_pieces, w_query, w_key, w_value, far_tables, token)
    if line:
        near_one = [sum_first(ends) for ends in near_ends]
        near_two = [sum_next(p, place, 2, q, q, token) for p, q in zip(near_parts, near_one)]
    heads, _ = attend_all(packed, facts[5:8])
    heads = lax.switch(
        far_mask,
        [
            lambda *pieces, there=by(bits): tuple(there(piece) for piece in pieces)
            for bits in range(data_size)
        ],
        *heads,
    )
    if line:
        earlier = [piece for pair in near_two for piece in pair]
        far_parts, far_ends, token = out_columns(heads, w_out, 2, line, earlier)
        near_three = [sum_next(p, place, 3, *q, token) for p, q in zip(near_parts, near_two)]
        far_one = [sum_first(ends) for ends in far_ends]
        far_two = [sum_next(p, place, 2, q, q, nothing) for p, q in zip(far_parts, far_one)]
        far_three = [sum_next(p, place, 3, *q, nothing) for p, q in zip(far_parts, far_two)]
        out_near = [add_rows(p, place, rows, *got) for p, got in zip(near_parts, near_three)]
        out_far = [add_rows(p, place, rows, *got) for p, got in zip(far_parts, far_three)]
    else:
        far_parts, _, _ = out_columns(heads, w_out, 1, line)
        out_near, out_far = [
            [lax.psum_scatter(part, "tensor", scatter_dimension=0, tiled=True) for part in parts]
            for parts in (near_parts, far_parts)
        ]
    out_near = jnp.concatenate(out_near, axis=1)
    out_far = jnp.concatenate(out_far, axis=1)
    return jnp.stack(
        [jnp.where(swap, out_near, out_far), jnp.where(swap, out_far, out_near)], axis=1
    )


def solution(mesh):
    placed = (
        P("tensor", "dp", None),
        P(),
        P(None, "tensor"),
        P(None, "tensor"),
        P(None, "tensor"),
        P("tensor", None),
        P("dp", None, "tensor"),
        P("dp", None, "tensor"),
        P(),
        P(),
        P(),
    )
    return jax.shard_map(
        local, mesh=mesh, in_specs=placed, out_specs=P("tensor", "dp", None), check_vma=False
    )
```

```python
import functools

import jax
import jax.numpy as jnp
from jax import lax
from jax.experimental import pallas as pl
from jax.experimental.pallas import tpu as pltpu
from jax.sharding import PartitionSpec as P

HD = 128
rope_base = 500000.0
norm_eps = 1e-05
masked = -1e30


def normalize(rows, norm_gain):
    floats = rows.astype(jnp.float32)
    return (
        floats * lax.rsqrt(jnp.mean(floats * floats, axis=-1, keepdims=True) + norm_eps) * norm_gain
    ).astype(jnp.bfloat16)


def rope_tables(first_position, span):
    half = HD // 2
    frequency = rope_base ** (-(jnp.arange(half, dtype=jnp.float32) * 2.0 / HD))
    positions = (first_position + jnp.arange(span, dtype=jnp.int32)).astype(jnp.float32)
    angles = positions[:, None] * frequency
    cosine = jnp.cos(angles)
    sine = jnp.sin(angles)
    return lax.optimization_barrier(
        (jnp.concatenate([cosine, cosine], axis=1), jnp.concatenate([-sine, sine], axis=1))
    )


def facts_kernel(per_device, slots_ref, spans_ref, prefixes_ref, out_ref):
    me = lax.axis_index("dp")
    base = me * per_device
    far = jnp.where(lax.div(slots_ref[base], per_device) ^ me == 1, 1, 0)
    far_mask = lax.div(slots_ref[base + far], per_device) ^ me
    out_ref[0] = far
    out_ref[1] = far_mask
    for start, mask in ((2, 1), (5, far_mask)):
        host = (me ^ mask) * per_device
        which = jnp.where(lax.div(slots_ref[host], per_device) == me, 0, 1)
        out_ref[start] = lax.rem(slots_ref[host + which], per_device)
        out_ref[start + 1] = prefixes_ref[host + which]
        out_ref[start + 2] = spans_ref[host + which]
    out_ref[8] = prefixes_ref[base + 1 - far]


def find_facts(slots, spans, prefixes, per_device):
    scalars = pl.BlockSpec(memory_space=pltpu.SMEM)
    return pl.pallas_call(
        functools.partial(facts_kernel, per_device),
        out_shape=jax.ShapeDtypeStruct((9,), jnp.int32),
        in_specs=[scalars] * 3,
        out_specs=scalars,
        name="find_facts",
    )(slots, spans, prefixes)


def project_kernel(chunk, kv_heads, groups, halves, sources, token_ref, *refs):
    count = halves * sources
    pieces = [refs[h * sources : (h + 1) * sources] for h in range(halves)]
    wq_hbm, wk_hbm, wv_hbm, cos_ref, sin_ref = refs[count : count + 5]
    out_ref, done_ref, x_ref, wq_ref, wk_ref, wv_ref, acc_ref, x_sems, sems = refs[count + 5 :]
    done_ref[0] = 0
    features = wq_hbm.shape[0]
    steps = features // chunk
    rows, width = pieces[0][0].shape
    place = lax.axis_index("tensor")

    def row_copies(half, act):
        columns = pl.ds(half * width, width)

        def copy(n, first):
            start = pl.multiple_of(first * rows, rows)
            act(
                pltpu.make_async_copy(
                    pieces[half][n], x_ref.at[pl.ds(start, pieces[half][n].shape[0]), columns],
                    x_sems.at[half, n],
                )
            )

        if sources == 1:
            copy(0, 0)
            return
        copy(0, place)
        for n, first, held in (
            (1, place - 1, place >= 1),
            (2, place + 1, place <= 2),
            (3, place - 2, place >= 2),
            (4, place + 2, place <= 1),
            (5, 3 - place, (place == 0) | (place == 3)),
        ):
            pl.when(held)(functools.partial(copy, n, first))

    def copies(index):
        piece = pl.ds(pl.multiple_of(index * chunk, chunk), chunk)
        return [
            pltpu.make_async_copy(source.at[piece, :], target.at[piece, :], sems.at[n, index])
            for n, (source, target) in enumerate(
                ((wq_hbm, wq_ref), (wk_hbm, wk_ref), (wv_hbm, wv_ref))
            )
        ]

    def begin(index, carry):
        for copy in copies(index):
            copy.start()
        return carry

    row_copies(0, lambda copy: copy.start())
    lax.fori_loop(0, 1, begin, 0)
    for half in range(1, halves):
        row_copies(half, lambda copy: copy.start())
    lax.fori_loop(1, steps, begin, 0)
    acc_ref[...] = jnp.zeros_like(acc_ref)

    def step(index, carry):
        for copy in copies(index):
            copy.wait()
        piece = pl.ds(pl.multiple_of(index * chunk, chunk), chunk)
        block = x_ref[:, piece]
        offset = 0
        for weights in (wq_ref, wk_ref, wv_ref):
            total = weights.shape[1]
            tile = min(256, total)
            for column in range(0, total, tile):
                acc_ref[:, offset + column : offset + column + tile] += jnp.dot(
                    block,
                    weights[piece, column : column + tile],
                    preferred_element_type=jnp.float32,
                )
            offset += total
        return carry

    each = steps // halves
    for half in range(halves):
        row_copies(half, lambda copy: copy.wait())
        lax.fori_loop(half * each, (half + 1) * each, step, 0)
    q_heads = kv_heads * groups
    for g in range(kv_heads):
        places = [g * groups + m for m in range(groups)] + [q_heads + g, q_heads + kv_heads + g]
        for slot, where in enumerate(places):
            part = acc_ref[:, where * HD : (where + 1) * HD]
            if slot <= groups:
                part = part * cos_ref[...] + pltpu.roll(part, HD // 2, 1) * sin_ref[...]
            start = (g * (groups + 2) + slot) * HD
            out_ref[:, start : start + HD] = part.astype(jnp.bfloat16)


def project(pieces, w_query, w_key, w_value, tables, token):
    span = tables[0].shape[0]
    features = w_query.shape[0]
    q_width, kv_width = w_query.shape[1], w_key.shape[1]
    kv_heads, groups = kv_width // HD, q_width // kv_width
    halves, sources = len(pieces), len(pieces[0])
    chunk = min(1024, features // halves)
    width = q_width + 2 * kv_width
    far_memory = pl.BlockSpec(memory_space=pltpu.HBM)
    here = pl.BlockSpec(memory_space=pltpu.VMEM)
    return pl.pallas_call(
        functools.partial(project_kernel, chunk, kv_heads, groups, halves, sources),
        out_shape=[
            jax.ShapeDtypeStruct((span, width), jnp.bfloat16),
            jax.ShapeDtypeStruct((1,), jnp.int32),
        ],
        in_specs=[pl.BlockSpec(memory_space=pltpu.SMEM)]
        + [far_memory] * (halves * sources + 3)
        + [here] * 2,
        out_specs=[here, pl.BlockSpec(memory_space=pltpu.SMEM)],
        scratch_shapes=[
            pltpu.VMEM((span, features), jnp.bfloat16),
            pltpu.VMEM((features, q_width), jnp.bfloat16),
            pltpu.VMEM((features, kv_width), jnp.bfloat16),
            pltpu.VMEM((features, kv_width), jnp.bfloat16),
            pltpu.VMEM((span, width), jnp.float32),
            pltpu.SemaphoreType.DMA((halves, sources)),
            pltpu.SemaphoreType.DMA((3, features // chunk)),
        ],
        compiler_params=pltpu.CompilerParams(vmem_limit_bytes=56 << 20),
        cost_estimate=pl.CostEstimate(flops=2 * span * features * width, bytes_accessed=2 * features * (width + span), transcendentals=0),
        name="project_rope",
    )(token, *[piece for half in pieces for piece in half], w_query, w_key, w_value, *tables)


def attend_kernel(
    kv_heads, block, facts, packed_ref, kc_hbm, vc_hbm, out_ref, done_ref,
    kc_ref, vc_ref, m_ref, acc_ref, ve_ref, sems,
):
    done_ref[0] = 0
    span = packed_ref.shape[0]
    each = packed_ref.shape[1] // kv_heads
    groups = each // HD - 2
    slot, prefix, length = facts[0], facts[1], facts[2]
    blocks = lax.div(prefix + (block - 1), block)
    factor = (HD**-0.5) * 1.4426950408889634
    contract = (((1,), (1,)), ((), ()))

    def copies(index):
        piece = pl.ds(pl.multiple_of(index * block, block), block)
        return [
            pltpu.make_async_copy(source.at[slot, piece, :], target.at[piece, :], sems.at[n, index])
            for n, (source, target) in enumerate(((kc_hbm, kc_ref), (vc_hbm, vc_ref)))
        ]

    def begin(index, carry):
        for copy in copies(index):
            copy.start()
        return carry

    lax.fori_loop(0, blocks, begin, 0)
    ve_ref[:, HD:] = jnp.ones((ve_ref.shape[0], HD), jnp.bfloat16)
    row = lax.broadcasted_iota(jnp.int32, (span, span), 0)
    column = lax.broadcasted_iota(jnp.int32, (span, span), 1)
    keep_new = (column <= row) & (column < length)

    def scores_of(g, keys, keep):
        scores = []
        for m in range(groups):
            start = g * each + m * HD
            query = packed_ref[:, start : start + HD]
            score = lax.dot_general(query, keys, contract, preferred_element_type=jnp.float32)
            scores.append(jnp.where(keep, score * factor, masked))
        return scores

    for g in range(kv_heads):
        start = g * each + groups * HD
        scores = scores_of(g, packed_ref[:, start : start + HD], keep_new)
        ve_ref[:span, :HD] = packed_ref[:, start + HD : start + 2 * HD]
        tops = [jnp.max(score, axis=1, keepdims=True) for score in scores]
        weights = [
            jnp.exp2(score - top).astype(jnp.bfloat16) for score, top in zip(scores, tops)
        ]
        for m in range(groups):
            head = g * groups + m
            m_ref[head] = jnp.broadcast_to(tops[m], (span, HD))
            acc_ref[head] = jnp.dot(
                weights[m], ve_ref[:span, :], preferred_element_type=jnp.float32
            )

    def step(index, carry):
        for copy in copies(index):
            copy.wait()
        start = pl.multiple_of(index * block, block)
        piece = pl.ds(start, block)
        keep = (start + lax.broadcasted_iota(jnp.int32, (1, block), 1)) < prefix
        for g in range(kv_heads):
            here = slice(g * HD, (g + 1) * HD)
            scores = scores_of(g, kc_ref[piece, here], keep)
            ve_ref[:block, :HD] = vc_ref[piece, here]
            before = [m_ref[g * groups + m] for m in range(groups)]
            tops = [
                jnp.maximum(old, jnp.max(score, axis=1, keepdims=True))
                for old, score in zip(before, scores)
            ]
            weights = [
                jnp.exp2(score - top[:, :1]).astype(jnp.bfloat16)
                for score, top in zip(scores, tops)
            ]
            for m in range(groups):
                head = g * groups + m
                shrink = jnp.exp2(before[m] - tops[m])
                m_ref[head] = tops[m]
                acc_ref[head] = acc_ref[head] * jnp.concatenate([shrink, shrink], axis=1) + jnp.dot(
                    weights[m], ve_ref[:block, :], preferred_element_type=jnp.float32
                )
        return carry

    lax.fori_loop(0, blocks, step, 0)
    for head in range(kv_heads * groups):
        total = acc_ref[head]
        out_ref[:, head * HD : (head + 1) * HD] = (total[:, :HD] / total[:, HD:]).astype(
            out_ref.dtype
        )


def attend(facts, packed, cache_keys, cache_values):
    span, width = packed.shape
    prefix, kv_width = cache_keys.shape[1:]
    kv_heads = kv_width // HD
    heads = width // HD - 2 * kv_heads
    block = min(1024, prefix)
    scalars = pl.BlockSpec(memory_space=pltpu.SMEM)
    here = pl.BlockSpec(memory_space=pltpu.VMEM)
    far_memory = pl.BlockSpec(memory_space=pltpu.HBM)
    return pl.pallas_call(
        functools.partial(attend_kernel, kv_heads, block),
        out_shape=[
            jax.ShapeDtypeStruct((span, heads * HD), jnp.bfloat16),
            jax.ShapeDtypeStruct((1,), jnp.int32),
        ],
        in_specs=[scalars, here, far_memory, far_memory],
        out_specs=[here, scalars],
        scratch_shapes=[
            pltpu.VMEM((prefix, kv_width), jnp.bfloat16),
            pltpu.VMEM((prefix, kv_width), jnp.bfloat16),
            pltpu.VMEM((heads, span, HD), jnp.float32),
            pltpu.VMEM((heads, span, 2 * HD), jnp.float32),
            pltpu.VMEM((max(block, span), 2 * HD), jnp.bfloat16),
            pltpu.SemaphoreType.DMA((2, prefix // block)),
        ],
        compiler_params=pltpu.CompilerParams(vmem_limit_bytes=56 << 20),
        cost_estimate=pl.CostEstimate(flops=1, bytes_accessed=1, transcendentals=0),
        name="attend_slot",
    )(facts, packed, cache_keys, cache_values)


def out_kernel(earlier, parts, line, tile, heads_ref, w_hbm, *refs):
    refs = refs[earlier:]
    outs = refs[:parts]
    firsts = refs[parts : 2 * parts] if line else ()
    done_ref, w_ref, sems = refs[-3:]
    done_ref[0] = 0
    columns = outs[0].shape[1]

    def copy(index):
        here = pl.ds(pl.multiple_of(index * tile, tile), tile)
        return pltpu.make_async_copy(w_hbm.at[:, here], w_ref.at[:, here], sems.at[index])

    def begin(index, carry):
        copy(index).start()
        return carry

    steps = columns // tile
    lax.fori_loop(0, parts * steps, begin, 0)
    if line:
        rows = firsts[0].shape[0]
        last = outs[0].shape[0] - rows
        start = pl.multiple_of(jnp.where(lax.axis_index("tensor") == 0, last, 0), rows)
    for part in range(parts):

        def step(index, carry):
            copy(index + part * steps).wait()
            there = pl.ds(pl.multiple_of((index + part * steps) * tile, tile), tile)
            here = pl.ds(pl.multiple_of(index * tile, tile), tile)
            total = jnp.dot(heads_ref[...], w_ref[:, there], preferred_element_type=jnp.float32)
            outs[part][:, here] = total.astype(outs[part].dtype)
            return carry

        lax.fori_loop(0, steps, step, 0)
        if line:
            firsts[part][...] = outs[part][pl.ds(start, rows), :]


def out_columns(heads, w_out, parts, line, earlier=()):
    span = heads.shape[0]
    inputs, columns = w_out.shape
    width = columns // parts
    tile = min(512, width)
    here = pl.BlockSpec(memory_space=pltpu.VMEM)
    far_memory = pl.BlockSpec(memory_space=pltpu.HBM)
    shapes = [jax.ShapeDtypeStruct((span, width), jnp.bfloat16)] * parts
    if line:
        shapes += [jax.ShapeDtypeStruct((span // 4, width), jnp.bfloat16)] * parts
    results = pl.pallas_call(
        functools.partial(out_kernel, len(earlier), parts, line, tile),
        out_shape=shapes + [jax.ShapeDtypeStruct((1,), jnp.int32)],
        in_specs=[here] + [far_memory] * (1 + len(earlier)),
        out_specs=[here] * len(shapes) + [pl.BlockSpec(memory_space=pltpu.SMEM)],
        scratch_shapes=[
            pltpu.VMEM((inputs, columns), jnp.bfloat16),
            pltpu.SemaphoreType.DMA((columns // tile,)),
        ],
        compiler_params=pltpu.CompilerParams(vmem_limit_bytes=56 << 20),
        cost_estimate=pl.CostEstimate(flops=1, bytes_accessed=1, transcendentals=0),
        name="out_columns",
    )(heads, w_out, *earlier)
    return results[:parts], results[parts:-1], results[-1]


def add_rows(partial, index, rows, *received):
    mine = lax.dynamic_slice_in_dim(partial, index * rows, rows, 0)
    if not received:
        return mine
    total = mine.astype(jnp.float32)
    for other in received:
        total = total + other.astype(jnp.float32)
    return total.astype(jnp.bfloat16)


def zero_after(*arrays):
    total = jnp.zeros((1,), jnp.float32)
    for array in arrays:
        total = total + jnp.minimum(jnp.abs(array[:1, 0].astype(jnp.float32)), 0.0)
    return total.astype(jnp.int32)


def gather_first(own):
    up = lax.ppermute(own, "tensor", [(0, 1), (1, 2), (2, 3)])
    down = lax.ppermute(own, "tensor", [(1, 0), (2, 1), (3, 2)])
    return up, down


def gather_second(up, down):
    up_two = lax.ppermute(up, "tensor", [(1, 2), (2, 3)])
    down_two = lax.ppermute(down, "tensor", [(1, 0), (2, 1)])
    return up_two, down_two


def gather_third(up_two, down_two, place):
    held = jnp.where(place >= 2, up_two, down_two)
    return lax.ppermute(held, "tensor", [(2, 3), (1, 0)])


def sum_first(ends):
    return lax.ppermute(ends, "tensor", [(0, 1), (3, 2)])


def sum_next(partial, place, step, up, down, token):
    place = place + token[0]
    rows = partial.shape[0] // 4
    sent_up = add_rows(partial, jnp.clip(place + 4 - step, 0, 3), rows, up)
    sent_down = add_rows(partial, jnp.clip(place - 4 + step, 0, 3), rows, down)
    return (
        lax.ppermute(sent_up, "tensor", [(a, a + 1) for a in range(step)]),
        lax.ppermute(sent_down, "tensor", [(a, a - 1) for a in range(4 - step, 4)]),
    )


def local(
    hidden_rows,
    norm_gain,
    w_query,
    w_key,
    w_value,
    w_out,
    cache_keys,
    cache_values,
    slot_of_request,
    span_length,
    prefix_length,
):
    data_size = lax.axis_size("dp")
    data_index = lax.axis_index("dp")
    tensor_size = lax.axis_size("tensor")
    place = lax.axis_index("tensor")
    rows, per_device, model = hidden_rows.shape
    span = rows * tensor_size
    q_width = w_query.shape[1]
    kv_width = w_key.shape[1]
    kv_heads = kv_width // HD
    line = tensor_size == 4
    cut = model // 2

    facts = find_facts(slot_of_request, span_length, prefix_length, per_device)
    far, far_mask = facts[0], facts[1]

    def by(bits):
        if bits == 0:
            return lambda values: values
        pairs = [(i, i ^ bits) for i in range(data_size)]
        return lambda values: lax.ppermute(values, "dp", pairs)

    near_by = by(1)

    nothing = jnp.zeros((1,), jnp.int32)
    swap = far == 1
    near_rows = jnp.where(swap, hidden_rows[:, 0, :], hidden_rows[:, 1, :])
    far_rows = jnp.where(swap, hidden_rows[:, 1, :], hidden_rows[:, 0, :])
    near_tables = rope_tables(facts[8], span)
    far_tables = rope_tables(facts[6], span)
    normed_near = normalize(near_rows, norm_gain)
    if line:

        def begin(bits):
            def run(rows, own):
                pieces = [own[:, c : c + cut] for c in (0, cut)]
                rows = by(bits)(rows)
                one = [gather_first(piece) for piece in pieces]
                two = [gather_second(*pair) for pair in one]
                three = [gather_third(*pair, place) for pair in two]
                gathered = [[p, *q, *r, t] for p, q, r, t in zip(pieces, one, two, three)]
                return gathered, normalize(rows, norm_gain)

            return run

        near_pieces, normed_far = lax.switch(
            far_mask, [begin(bits) for bits in range(data_size)], far_rows, normed_near
        )
        far_one = gather_first(normed_far)
    else:
        near_pieces = [[lax.all_gather(normed_near, "tensor", axis=0, tiled=True)]]
        far_rows = lax.switch(far_mask, [by(bits) for bits in range(data_size)], far_rows)
        normed_far = normalize(far_rows, norm_gain)
        far_pieces = [[lax.all_gather(normed_far, "tensor", axis=0, tiled=True)]]
    packed, token = project(near_pieces, w_query, w_key, w_value, near_tables, nothing)
    if line:
        behind = token[0].astype(jnp.bfloat16)
        far_two = gather_second(*(piece + behind for piece in far_one))
    heads, token = attend(facts[2:5], near_by(packed), cache_keys, cache_values)
    if line:
        far_three = gather_third(*far_two, place + token[0])
        far_pieces = [[normed_far, *far_one, *far_two, far_three]]
    near_parts, near_ends, token = out_columns(near_by(heads), w_out, 1, line)
    packed, token = project(far_pieces, w_query, w_key, w_value, far_tables, token)
    if line:
        near_one = [sum_first(ends) for ends in near_ends]
        near_two = [sum_next(p, place, 2, q, q, token) for p, q in zip(near_parts, near_one)]
    heads, _ = attend(facts[5:8], packed, cache_keys, cache_values)
    heads = lax.switch(far_mask, [by(bits) for bits in range(data_size)], heads)
    if line:
        earlier = [piece for pair in near_two for piece in pair]
        far_parts, far_ends, token = out_columns(heads, w_out, 2, line, earlier)
        behind = zero_after(heads)
        near_three = [sum_next(p, place, 3, *q, behind) for p, q in zip(near_parts, near_two)]
        far_one = [sum_first(ends) for ends in far_ends]
        behind = zero_after(*[piece for pair in near_three for piece in pair])
        far_two = [sum_next(p, place, 2, q, q, behind) for p, q in zip(far_parts, far_one)]
        far_three = [sum_next(p, place, 3, *q, nothing) for p, q in zip(far_parts, far_two)]
        out_near = [add_rows(p, place, rows, *got) for p, got in zip(near_parts, near_three)]
        out_far = [add_rows(p, place, rows, *got) for p, got in zip(far_parts, far_three)]
    else:
        far_parts, _, _ = out_columns(heads, w_out, 1, line)
        out_near, out_far = [
            [lax.psum_scatter(part, "tensor", scatter_dimension=0, tiled=True) for part in parts]
            for parts in (near_parts, far_parts)
        ]
    out_near = jnp.concatenate(out_near, axis=1)
    out_far = jnp.concatenate(out_far, axis=1)
    return jnp.stack(
        [jnp.where(swap, out_near, out_far), jnp.where(swap, out_far, out_near)], axis=1
    )


def solution(mesh):
    placed = (
        P("tensor", "dp", None),
        P(),
        P(None, "tensor"),
        P(None, "tensor"),
        P(None, "tensor"),
        P("tensor", None),
        P("dp", None, "tensor"),
        P("dp", None, "tensor"),
        P(),
        P(),
        P(),
    )
    return jax.shard_map(
        local, mesh=mesh, in_specs=placed, out_specs=P("tensor", "dp", None), check_vma=False
    )
```

```python
import functools

import jax
import jax.numpy as jnp
from jax import lax
from jax.experimental import pallas as pl
from jax.experimental.pallas import tpu as pltpu
from jax.sharding import PartitionSpec as P

HD = 128
rope_base = 500000.0
norm_eps = 1e-05
masked = -1e30


def normalize(rows, norm_gain):
    floats = rows.astype(jnp.float32)
    return (
        floats * lax.rsqrt(jnp.mean(floats * floats, axis=-1, keepdims=True) + norm_eps) * norm_gain
    ).astype(jnp.bfloat16)


def rope_rates():
    half = HD // 2
    frequency = rope_base ** (-(jnp.arange(half, dtype=jnp.float32) * 2.0 / HD))
    return jnp.concatenate([frequency, frequency])[None, :]


def facts_kernel(per_device, slots_ref, spans_ref, prefixes_ref, out_ref):
    me = lax.axis_index("dp")
    base = me * per_device
    far = jnp.where(lax.div(slots_ref[base], per_device) ^ me == 1, 1, 0)
    far_mask = lax.div(slots_ref[base + far], per_device) ^ me
    host = (me ^ far_mask) * per_device
    guest = host + jnp.where(lax.div(slots_ref[host], per_device) == me, 0, 1)
    near = base + 1 - far
    out_ref[0] = far
    out_ref[1] = far_mask
    out_ref[2] = lax.rem(slots_ref[guest], per_device)
    out_ref[3] = lax.rem(slots_ref[near], per_device)
    out_ref[4] = prefixes_ref[near]
    out_ref[5] = spans_ref[near]
    out_ref[6] = 0
    out_ref[7] = prefixes_ref[base + far]
    out_ref[8] = spans_ref[base + far]


def find_facts(slots, spans, prefixes, per_device):
    scalars = pl.BlockSpec(memory_space=pltpu.SMEM)
    return pl.pallas_call(
        functools.partial(facts_kernel, per_device),
        out_shape=jax.ShapeDtypeStruct((9,), jnp.int32),
        in_specs=[scalars] * 3,
        out_specs=scalars,
        name="find_facts",
    )(slots, spans, prefixes)


def project_kernel(chunk, kv_heads, groups, halves, sources, earlier, first_ref, token_ref, *refs):
    count = halves * sources
    pieces = [refs[h * sources : (h + 1) * sources] for h in range(halves)]
    wq_hbm, wk_hbm, wv_hbm, rates_ref = refs[count : count + 4]
    refs = refs[count + 4 + earlier :]
    out_ref, done_ref, x_ref, wq_ref, wk_ref, wv_ref, acc_ref, cos_ref, sin_ref, x_sems, sems = refs
    done_ref[0] = 0
    done_ref[0] = 0
    features = wq_hbm.shape[0]
    steps = features // chunk
    rows, width = pieces[0][0].shape
    place = lax.axis_index("tensor")

    def row_copies(half, act):
        columns = pl.ds(half * width, width)

        def copy(n, first):
            start = pl.multiple_of(first * rows, rows)
            act(
                pltpu.make_async_copy(
                    pieces[half][n], x_ref.at[pl.ds(start, pieces[half][n].shape[0]), columns],
                    x_sems.at[half, n],
                )
            )

        if sources == 1:
            copy(0, 0)
            return
        copy(0, place)
        for n, first, held in (
            (1, place - 1, place >= 1),
            (2, place + 1, place <= 2),
            (3, place - 2, place >= 2),
            (4, place + 2, place <= 1),
            (5, 3 - place, (place == 0) | (place == 3)),
        ):
            pl.when(held)(functools.partial(copy, n, first))

    def copies(index):
        piece = pl.ds(pl.multiple_of(index * chunk, chunk), chunk)
        return [
            pltpu.make_async_copy(source.at[piece, :], target.at[piece, :], sems.at[n, index])
            for n, (source, target) in enumerate(
                ((wq_hbm, wq_ref), (wk_hbm, wk_ref), (wv_hbm, wv_ref))
            )
        ]

    def begin(index, carry):
        for copy in copies(index):
            copy.start()
        return carry

    row_copies(0, lambda copy: copy.start())
    lax.fori_loop(0, 1, begin, 0)
    for half in range(1, halves):
        row_copies(half, lambda copy: copy.start())
    lax.fori_loop(1, steps, begin, 0)
    acc_ref[...] = jnp.zeros_like(acc_ref)
    row = lax.broadcasted_iota(jnp.int32, cos_ref.shape, 0)
    lane = lax.broadcasted_iota(jnp.int32, cos_ref.shape, 1)
    angles = (first_ref[0] + row).astype(jnp.float32) * rates_ref[...]
    cos_ref[...] = jnp.cos(angles)
    sin_ref[...] = jnp.where(lane < HD // 2, -1.0, 1.0) * jnp.sin(angles)

    def step(index, carry):
        for copy in copies(index):
            copy.wait()
        piece = pl.ds(pl.multiple_of(index * chunk, chunk), chunk)
        block = x_ref[:, piece]
        offset = 0
        for weights in (wq_ref, wk_ref, wv_ref):
            total = weights.shape[1]
            tile = min(256, total)
            for column in range(0, total, tile):
                acc_ref[:, offset + column : offset + column + tile] += jnp.dot(
                    block,
                    weights[piece, column : column + tile],
                    preferred_element_type=jnp.float32,
                )
            offset += total
        return carry

    each = steps // halves
    for half in range(halves):
        row_copies(half, lambda copy: copy.wait())
        lax.fori_loop(half * each, (half + 1) * each, step, 0)
    q_heads = kv_heads * groups
    for g in range(kv_heads):
        places = [g * groups + m for m in range(groups)] + [q_heads + g, q_heads + kv_heads + g]
        for slot, where in enumerate(places):
            part = acc_ref[:, where * HD : (where + 1) * HD]
            if slot <= groups:
                part = part * cos_ref[...] + pltpu.roll(part, HD // 2, 1) * sin_ref[...]
            start = (g * (groups + 2) + slot) * HD
            out_ref[:, start : start + HD] = part.astype(jnp.bfloat16)


def project(pieces, w_query, w_key, w_value, first_position, token, span, earlier=()):
    features = w_query.shape[0]
    q_width, kv_width = w_query.shape[1], w_key.shape[1]
    kv_heads, groups = kv_width // HD, q_width // kv_width
    halves, sources = len(pieces), len(pieces[0])
    chunk = min(1024, features // halves)
    width = q_width + 2 * kv_width
    far_memory = pl.BlockSpec(memory_space=pltpu.HBM)
    here = pl.BlockSpec(memory_space=pltpu.VMEM)
    return pl.pallas_call(
        functools.partial(project_kernel, chunk, kv_heads, groups, halves, sources, len(earlier)),
        out_shape=[
            jax.ShapeDtypeStruct((span, width), jnp.bfloat16),
            jax.ShapeDtypeStruct((1,), jnp.int32),
        ],
        in_specs=[pl.BlockSpec(memory_space=pltpu.SMEM)] * 2
        + [far_memory] * (halves * sources + 3)
        + [here]
        + [far_memory] * len(earlier),
        out_specs=[here, pl.BlockSpec(memory_space=pltpu.SMEM)],
        scratch_shapes=[
            pltpu.VMEM((span, features), jnp.bfloat16),
            pltpu.VMEM((features, q_width), jnp.bfloat16),
            pltpu.VMEM((features, kv_width), jnp.bfloat16),
            pltpu.VMEM((features, kv_width), jnp.bfloat16),
            pltpu.VMEM((span, width), jnp.float32),
            pltpu.VMEM((span, HD), jnp.float32),
            pltpu.VMEM((span, HD), jnp.float32),
            pltpu.SemaphoreType.DMA((halves, sources)),
            pltpu.SemaphoreType.DMA((3, features // chunk)),
        ],
        compiler_params=pltpu.CompilerParams(vmem_limit_bytes=56 << 20),
        cost_estimate=pl.CostEstimate(flops=1, bytes_accessed=1, transcendentals=0),
        name="project_rope",
    )(
        first_position, token, *[piece for half in pieces for piece in half],
        w_query, w_key, w_value, rope_rates(), *earlier,
    )


def attend_kernel(
    kv_heads, block, facts, packed_ref, kc_hbm, vc_hbm, out_ref, done_ref,
    kc_ref, vc_ref, m_ref, acc_ref, ve_ref, sems,
):
    done_ref[0] = 0
    span = packed_ref.shape[0]
    each = packed_ref.shape[1] // kv_heads
    groups = each // HD - 2
    slot, prefix, length = facts[0], facts[1], facts[2]
    blocks = lax.div(prefix + (block - 1), block)
    factor = (HD**-0.5) * 1.4426950408889634
    contract = (((1,), (1,)), ((), ()))

    def copies(index):
        piece = pl.ds(pl.multiple_of(index * block, block), block)
        return [
            pltpu.make_async_copy(source.at[slot, piece, :], target.at[piece, :], sems.at[n, index])
            for n, (source, target) in enumerate(((kc_hbm, kc_ref), (vc_hbm, vc_ref)))
        ]

    def begin(index, carry):
        for copy in copies(index):
            copy.start()
        return carry

    lax.fori_loop(0, blocks, begin, 0)
    ve_ref[:, HD:] = jnp.ones((ve_ref.shape[0], HD), jnp.bfloat16)
    row = lax.broadcasted_iota(jnp.int32, (span, span), 0)
    column = lax.broadcasted_iota(jnp.int32, (span, span), 1)
    keep_new = (column <= row) & (column < length)

    def scores_of(g, keys, keep):
        scores = []
        for m in range(groups):
            start = g * each + m * HD
            query = packed_ref[:, start : start + HD]
            score = lax.dot_general(query, keys, contract, preferred_element_type=jnp.float32)
            scores.append(jnp.where(keep, score * factor, masked))
        return scores

    for g in range(kv_heads):
        start = g * each + groups * HD
        scores = scores_of(g, packed_ref[:, start : start + HD], keep_new)
        ve_ref[:span, :HD] = packed_ref[:, start + HD : start + 2 * HD]
        tops = [jnp.max(score, axis=1, keepdims=True) for score in scores]
        weights = [
            jnp.exp2(score - top).astype(jnp.bfloat16) for score, top in zip(scores, tops)
        ]
        for m in range(groups):
            head = g * groups + m
            m_ref[head] = jnp.broadcast_to(tops[m], (span, HD))
            acc_ref[head] = jnp.dot(
                weights[m], ve_ref[:span, :], preferred_element_type=jnp.float32
            )

    def step(index, carry):
        for copy in copies(index):
            copy.wait()
        start = pl.multiple_of(index * block, block)
        piece = pl.ds(start, block)
        keep = (start + lax.broadcasted_iota(jnp.int32, (1, block), 1)) < prefix
        for g in range(kv_heads):
            here = slice(g * HD, (g + 1) * HD)
            scores = scores_of(g, kc_ref[piece, here], keep)
            ve_ref[:block, :HD] = vc_ref[piece, here]
            before = [m_ref[g * groups + m] for m in range(groups)]
            tops = [
                jnp.maximum(old, jnp.max(score, axis=1, keepdims=True))
                for old, score in zip(before, scores)
            ]
            weights = [
                jnp.exp2(score - top[:, :1]).astype(jnp.bfloat16)
                for score, top in zip(scores, tops)
            ]
            for m in range(groups):
                head = g * groups + m
                shrink = jnp.exp2(before[m] - tops[m])
                m_ref[head] = tops[m]
                acc_ref[head] = acc_ref[head] * jnp.concatenate([shrink, shrink], axis=1) + jnp.dot(
                    weights[m], ve_ref[:block, :], preferred_element_type=jnp.float32
                )
        return carry

    lax.fori_loop(0, blocks, step, 0)
    for head in range(kv_heads * groups):
        total = acc_ref[head]
        out_ref[:, head * HD : (head + 1) * HD] = (total[:, :HD] / total[:, HD:]).astype(
            out_ref.dtype
        )


def attend(facts, packed, cache_keys, cache_values):
    span, width = packed.shape
    prefix, kv_width = cache_keys.shape[1:]
    kv_heads = kv_width // HD
    heads = width // HD - 2 * kv_heads
    block = min(1024, prefix)
    scalars = pl.BlockSpec(memory_space=pltpu.SMEM)
    here = pl.BlockSpec(memory_space=pltpu.VMEM)
    far_memory = pl.BlockSpec(memory_space=pltpu.HBM)
    return pl.pallas_call(
        functools.partial(attend_kernel, kv_heads, block),
        out_shape=[
            jax.ShapeDtypeStruct((span, heads * HD), jnp.bfloat16),
            jax.ShapeDtypeStruct((1,), jnp.int32),
        ],
        in_specs=[scalars, here, far_memory, far_memory],
        out_specs=[here, scalars],
        scratch_shapes=[
            pltpu.VMEM((prefix, kv_width), jnp.bfloat16),
            pltpu.VMEM((prefix, kv_width), jnp.bfloat16),
            pltpu.VMEM((heads, span, HD), jnp.float32),
            pltpu.VMEM((heads, span, 2 * HD), jnp.float32),
            pltpu.VMEM((max(block, span), 2 * HD), jnp.bfloat16),
            pltpu.SemaphoreType.DMA((2, prefix // block)),
        ],
        compiler_params=pltpu.CompilerParams(vmem_limit_bytes=56 << 20),
        cost_estimate=pl.CostEstimate(flops=1, bytes_accessed=1, transcendentals=0),
        name="attend_slot",
    )(facts, packed, cache_keys, cache_values)


def out_kernel(earlier, parts, line, tile, heads_ref, w_hbm, *refs):
    refs = refs[earlier:]
    outs = refs[:parts]
    firsts = refs[parts : 2 * parts] if line else ()
    done_ref, w_ref, sems = refs[-3:]
    done_ref[0] = 0
    columns = outs[0].shape[1]

    def copy(index):
        here = pl.ds(pl.multiple_of(index * tile, tile), tile)
        return pltpu.make_async_copy(w_hbm.at[:, here], w_ref.at[:, here], sems.at[index])

    def begin(index, carry):
        copy(index).start()
        return carry

    steps = columns // tile
    lax.fori_loop(0, parts * steps, begin, 0)
    if line:
        rows = firsts[0].shape[0]
        place = lax.axis_index("tensor")
        start = pl.multiple_of(jnp.where(place == 0, 3, 0) * rows, rows)
    for part in range(parts):

        def step(index, carry):
            copy(index + part * steps).wait()
            there = pl.ds(pl.multiple_of((index + part * steps) * tile, tile), tile)
            here = pl.ds(pl.multiple_of(index * tile, tile), tile)
            total = jnp.dot(heads_ref[...], w_ref[:, there], preferred_element_type=jnp.float32)
            outs[part][:, here] = total.astype(outs[part].dtype)
            return carry

        lax.fori_loop(0, steps, step, 0)
        if line:
            firsts[part][...] = outs[part][pl.ds(start, rows), :]


def out_columns(heads, w_out, parts, line, earlier=()):
    span = heads.shape[0]
    inputs, columns = w_out.shape
    width = columns // parts
    tile = min(512, width)
    here = pl.BlockSpec(memory_space=pltpu.VMEM)
    far_memory = pl.BlockSpec(memory_space=pltpu.HBM)
    shapes = [jax.ShapeDtypeStruct((span, width), jnp.bfloat16)] * parts
    if line:
        shapes += [jax.ShapeDtypeStruct((span // 4, width), jnp.bfloat16)] * parts
    results = pl.pallas_call(
        functools.partial(out_kernel, len(earlier), parts, line, tile),
        out_shape=shapes + [jax.ShapeDtypeStruct((1,), jnp.int32)],
        in_specs=[here] + [far_memory] * (1 + len(earlier)),
        out_specs=[here] * len(shapes) + [pl.BlockSpec(memory_space=pltpu.SMEM)],
        scratch_shapes=[
            pltpu.VMEM((inputs, columns), jnp.bfloat16),
            pltpu.SemaphoreType.DMA((columns // tile,)),
        ],
        compiler_params=pltpu.CompilerParams(vmem_limit_bytes=56 << 20),
        cost_estimate=pl.CostEstimate(flops=1, bytes_accessed=1, transcendentals=0),
        name="out_columns",
    )(heads, w_out, *earlier)
    return results[:parts], results[parts:-1], results[-1]


def add_rows(partial, index, rows, *received):
    mine = lax.dynamic_slice_in_dim(partial, index * rows, rows, 0)
    if not received:
        return mine
    total = mine.astype(jnp.float32)
    for other in received:
        total = total + other.astype(jnp.float32)
    return total.astype(jnp.bfloat16)


def zero_after(*arrays):
    total = jnp.zeros((1,), jnp.float32)
    for array in arrays:
        total = total + jnp.minimum(jnp.abs(array[:1, 0].astype(jnp.float32)), 0.0)
    return total.astype(jnp.int32)


def gather_first(own):
    up = lax.ppermute(own, "tensor", [(0, 1), (1, 2), (2, 3)])
    down = lax.ppermute(own, "tensor", [(1, 0), (2, 1), (3, 2)])
    return up, down


def gather_second(up, down):
    up_two = lax.ppermute(up, "tensor", [(1, 2), (2, 3)])
    down_two = lax.ppermute(down, "tensor", [(1, 0), (2, 1)])
    return up_two, down_two


def gather_third(up_two, down_two, place):
    held = jnp.where(place >= 2, up_two, down_two)
    return lax.ppermute(held, "tensor", [(2, 3), (1, 0)])


def sum_first(ends):
    return lax.ppermute(ends, "tensor", [(0, 1), (3, 2)])


def sum_second(partial, place, received):
    rows = partial.shape[0] // 4
    sent = add_rows(partial, jnp.where(place <= 1, place + 2, place - 2), rows, received)
    return (
        lax.ppermute(sent, "tensor", [(0, 1), (1, 2)]),
        lax.ppermute(sent, "tensor", [(3, 2), (2, 1)]),
    )


def sum_third(partial, place, up, down, token):
    rows = partial.shape[0] // 4
    place = place + token[0]
    sent_up = add_rows(partial, jnp.minimum(place + 1, 3), rows, up)
    sent_down = add_rows(partial, jnp.maximum(place - 1, 0), rows, down)
    return (
        lax.ppermute(sent_up, "tensor", [(0, 1), (1, 2), (2, 3)]),
        lax.ppermute(sent_down, "tensor", [(1, 0), (2, 1), (3, 2)]),
    )


def local(
    hidden_rows,
    norm_gain,
    w_query,
    w_key,
    w_value,
    w_out,
    cache_keys,
    cache_values,
    slot_of_request,
    span_length,
    prefix_length,
):
    data_size = lax.axis_size("dp")
    data_index = lax.axis_index("dp")
    tensor_size = lax.axis_size("tensor")
    place = lax.axis_index("tensor")
    rows, per_device, model = hidden_rows.shape
    span = rows * tensor_size
    q_width = w_query.shape[1]
    kv_width = w_key.shape[1]
    kv_heads = kv_width // HD
    line = tensor_size == 4
    cut = model // 2

    facts = find_facts(slot_of_request, span_length, prefix_length, per_device)
    far, far_mask = facts[0], facts[1]

    def by(bits):
        if bits == 0:
            return lambda values: values
        pairs = [(i, i ^ bits) for i in range(data_size)]
        return lambda values: lax.ppermute(values, "dp", pairs)

    nothing = jnp.zeros((1,), jnp.int32)
    swap = far == 1
    near_rows = jnp.where(swap, hidden_rows[:, 0, :], hidden_rows[:, 1, :])
    far_rows = jnp.where(swap, hidden_rows[:, 1, :], hidden_rows[:, 0, :])
    normed_near = normalize(near_rows, norm_gain)

    def caches_by(bits):
        def run(slot, *caches):
            lent = [lax.dynamic_index_in_dim(cache, slot, 0, True) for cache in caches]
            return [by(1)(cache) for cache in caches], [by(bits)(cache) for cache in lent]

        return run

    if line:

        def begin(bits):
            def run(rows, own, slot, cache_keys, cache_values):
                pieces = [own[:, c : c + cut] for c in (0, cut)]
                one = [gather_first(piece) for piece in pieces]
                caches = caches_by(bits)(slot, cache_keys, cache_values)
                two = [gather_second(*pair) for pair in one]
                three = [gather_third(*pair, place) for pair in two]
                gathered = [[p, *q, *r, t] for p, q, r, t in zip(pieces, one, two, three)]
                return gathered, normalize(rows, norm_gain), caches

            return run

        near_pieces, normed_far, (near_caches, far_caches) = lax.switch(
            far_mask,
            [begin(bits) for bits in range(data_size)],
            far_rows,
            normed_near,
            facts[2],
            cache_keys,
            cache_values,
        )
        far_one = gather_first(normed_far)
    else:
        near_pieces = [[lax.all_gather(normed_near, "tensor", axis=0, tiled=True)]]
        near_caches, far_caches = lax.switch(
            far_mask, [caches_by(bits) for bits in range(data_size)], facts[2], cache_keys, cache_values
        )
        normed_far = normalize(far_rows, norm_gain)
        far_pieces = [[lax.all_gather(normed_far, "tensor", axis=0, tiled=True)]]
    weights = w_query, w_key, w_value
    packed, token = project(near_pieces, *weights, facts[4:5], nothing, span)
    heads, token = attend(facts[3:6], packed, *near_caches)
    if line:
        behind = token[0].astype(jnp.bfloat16)
        far_two = gather_second(*(piece + behind for piece in far_one))
    near_parts, near_ends, token = out_columns(heads, w_out, 1, line)
    earlier = []
    if line:
        near_one = sum_first(near_ends[0])
        far_three = gather_third(*far_two, place + token[0])
        far_pieces = [[normed_far, *far_one, *far_two, far_three]]
        near_two = sum_second(near_parts[0], place, near_one)
        earlier = [near_one]
    packed, token = project(far_pieces, *weights, facts[7:8], nothing, span, earlier)
    heads, token = attend(facts[6:9], packed, *far_caches)
    if line:
        near_three = sum_third(near_parts[0], place, *near_two, token)
        far_parts, far_ends, _ = out_columns(heads, w_out, 2, line, near_two)
        far_one = [sum_first(ends) for ends in far_ends]
        behind = zero_after(*near_three)
        far_two = [sum_second(p, place + behind[0], q) for p, q in zip(far_parts, far_one)]
        far_three = [sum_third(p, place, *q, nothing) for p, q in zip(far_parts, far_two)]
        out_near = [add_rows(near_parts[0], place, rows, *near_three)]
        out_far = [add_rows(p, place, rows, *got) for p, got in zip(far_parts, far_three)]
    else:
        far_parts, _, _ = out_columns(heads, w_out, 1, line)
        out_near, out_far = [
            [lax.psum_scatter(part, "tensor", scatter_dimension=0, tiled=True) for part in parts]
            for parts in (near_parts, far_parts)
        ]
    out_near = jnp.concatenate(out_near, axis=1)
    out_far = jnp.concatenate(out_far, axis=1)
    return jnp.stack(
        [jnp.where(swap, out_near, out_far), jnp.where(swap, out_far, out_near)], axis=1
    )


def solution(mesh):
    placed = (
        P("tensor", "dp", None),
        P(),
        P(None, "tensor"),
        P(None, "tensor"),
        P(None, "tensor"),
        P("tensor", None),
        P("dp", None, "tensor"),
        P("dp", None, "tensor"),
        P(),
        P(),
        P(),
    )
    return jax.shard_map(
        local, mesh=mesh, in_specs=placed, out_specs=P("tensor", "dp", None), check_vma=False
    )
```

```python
import functools

import jax
import jax.numpy as jnp
from jax import lax
from jax.experimental import pallas as pl
from jax.experimental.pallas import tpu as pltpu
from jax.sharding import PartitionSpec as P

HD = 128
rope_base = 500000.0
norm_eps = 1e-05
masked = -1e30


def normalize(rows, norm_gain):
    floats = rows.astype(jnp.float32)
    return (
        floats * lax.rsqrt(jnp.mean(floats * floats, axis=-1, keepdims=True) + norm_eps) * norm_gain
    ).astype(jnp.bfloat16)


def rope_rates():
    half = HD // 2
    frequency = rope_base ** (-(jnp.arange(half, dtype=jnp.float32) * 2.0 / HD))
    return jnp.concatenate([frequency, frequency])[None, :]


def facts_kernel(per_device, slots_ref, spans_ref, prefixes_ref, out_ref):
    me = lax.axis_index("dp")
    base = me * per_device
    far = jnp.where(lax.div(slots_ref[base], per_device) ^ me == 1, 1, 0)
    far_mask = lax.div(slots_ref[base + far], per_device) ^ me
    host = (me ^ far_mask) * per_device
    guest = host + jnp.where(lax.div(slots_ref[host], per_device) == me, 0, 1)
    near = base + 1 - far
    out_ref[0] = far
    out_ref[1] = far_mask
    out_ref[2] = lax.rem(slots_ref[guest], per_device)
    out_ref[3] = lax.rem(slots_ref[near], per_device)
    out_ref[4] = prefixes_ref[near]
    out_ref[5] = spans_ref[near]
    out_ref[6] = 0
    out_ref[7] = 0
    out_ref[8] = prefixes_ref[base + far]
    out_ref[9] = spans_ref[base + far]
    out_ref[10] = far_mask & 1


def find_facts(slots, spans, prefixes, per_device):
    scalars = pl.BlockSpec(memory_space=pltpu.SMEM)
    return pl.pallas_call(
        functools.partial(facts_kernel, per_device),
        out_shape=jax.ShapeDtypeStruct((11,), jnp.int32),
        in_specs=[scalars] * 3,
        out_specs=scalars,
        name="find_facts",
    )(slots, spans, prefixes)


def project_kernel(chunk, kv_heads, groups, halves, sources, earlier, first_ref, token_ref, *refs):
    count = halves * sources
    pieces = [refs[h * sources : (h + 1) * sources] for h in range(halves)]
    wq_hbm, wk_hbm, wv_hbm, rates_ref = refs[count : count + 4]
    refs = refs[count + 4 + earlier :]
    out_ref, done_ref, x_ref, wq_ref, wk_ref, wv_ref, acc_ref, cos_ref, sin_ref, x_sems, sems = refs
    done_ref[0] = 0
    done_ref[0] = 0
    features = wq_hbm.shape[0]
    steps = features // chunk
    rows, width = pieces[0][0].shape
    place = lax.axis_index("tensor")

    def row_copies(half, act):
        columns = pl.ds(half * width, width)

        def copy(n, first):
            start = pl.multiple_of(first * rows, rows)
            act(
                pltpu.make_async_copy(
                    pieces[half][n], x_ref.at[pl.ds(start, pieces[half][n].shape[0]), columns],
                    x_sems.at[half, n],
                )
            )

        if sources == 1:
            copy(0, 0)
            return
        copy(0, place)
        for n, first, held in (
            (1, place - 1, place >= 1),
            (2, place + 1, place <= 2),
            (3, place - 2, place >= 2),
            (4, place + 2, place <= 1),
            (5, 3 - place, (place == 0) | (place == 3)),
        ):
            pl.when(held)(functools.partial(copy, n, first))

    def copies(index):
        piece = pl.ds(pl.multiple_of(index * chunk, chunk), chunk)
        return [
            pltpu.make_async_copy(source.at[piece, :], target.at[piece, :], sems.at[n, index])
            for n, (source, target) in enumerate(
                ((wq_hbm, wq_ref), (wk_hbm, wk_ref), (wv_hbm, wv_ref))
            )
        ]

    def begin(index, carry):
        for copy in copies(index):
            copy.start()
        return carry

    row_copies(0, lambda copy: copy.start())
    lax.fori_loop(0, 1, begin, 0)
    for half in range(1, halves):
        row_copies(half, lambda copy: copy.start())
    lax.fori_loop(1, steps, begin, 0)
    acc_ref[...] = jnp.zeros_like(acc_ref)
    row = lax.broadcasted_iota(jnp.int32, cos_ref.shape, 0)
    lane = lax.broadcasted_iota(jnp.int32, cos_ref.shape, 1)
    angles = (first_ref[0] + row).astype(jnp.float32) * rates_ref[...]
    cos_ref[...] = jnp.cos(angles)
    sin_ref[...] = jnp.where(lane < HD // 2, -1.0, 1.0) * jnp.sin(angles)

    def step(index, carry):
        for copy in copies(index):
            copy.wait()
        piece = pl.ds(pl.multiple_of(index * chunk, chunk), chunk)
        block = x_ref[:, piece]
        offset = 0
        for weights in (wq_ref, wk_ref, wv_ref):
            total = weights.shape[1]
            tile = min(256, total)
            for column in range(0, total, tile):
                acc_ref[:, offset + column : offset + column + tile] += jnp.dot(
                    block,
                    weights[piece, column : column + tile],
                    preferred_element_type=jnp.float32,
                )
            offset += total
        return carry

    each = steps // halves
    for half in range(halves):
        row_copies(half, lambda copy: copy.wait())
        lax.fori_loop(half * each, (half + 1) * each, step, 0)
    q_heads = kv_heads * groups
    for g in range(kv_heads):
        places = [g * groups + m for m in range(groups)] + [q_heads + g, q_heads + kv_heads + g]
        for slot, where in enumerate(places):
            part = acc_ref[:, where * HD : (where + 1) * HD]
            if slot <= groups:
                part = part * cos_ref[...] + pltpu.roll(part, HD // 2, 1) * sin_ref[...]
            start = (g * (groups + 2) + slot) * HD
            out_ref[:, start : start + HD] = part.astype(jnp.bfloat16)


def project(pieces, w_query, w_key, w_value, first_position, token, span, earlier=()):
    features = w_query.shape[0]
    q_width, kv_width = w_query.shape[1], w_key.shape[1]
    kv_heads, groups = kv_width // HD, q_width // kv_width
    halves, sources = len(pieces), len(pieces[0])
    chunk = min(1024, features // halves)
    width = q_width + 2 * kv_width
    far_memory = pl.BlockSpec(memory_space=pltpu.HBM)
    here = pl.BlockSpec(memory_space=pltpu.VMEM)
    return pl.pallas_call(
        functools.partial(project_kernel, chunk, kv_heads, groups, halves, sources, len(earlier)),
        out_shape=[
            jax.ShapeDtypeStruct((span, width), jnp.bfloat16),
            jax.ShapeDtypeStruct((1,), jnp.int32),
        ],
        in_specs=[pl.BlockSpec(memory_space=pltpu.SMEM)] * 2
        + [far_memory] * (halves * sources + 3)
        + [here]
        + [far_memory] * len(earlier),
        out_specs=[here, pl.BlockSpec(memory_space=pltpu.SMEM)],
        scratch_shapes=[
            pltpu.VMEM((span, features), jnp.bfloat16),
            pltpu.VMEM((features, q_width), jnp.bfloat16),
            pltpu.VMEM((features, kv_width), jnp.bfloat16),
            pltpu.VMEM((features, kv_width), jnp.bfloat16),
            pltpu.VMEM((span, width), jnp.float32),
            pltpu.VMEM((span, HD), jnp.float32),
            pltpu.VMEM((span, HD), jnp.float32),
            pltpu.SemaphoreType.DMA((halves, sources)),
            pltpu.SemaphoreType.DMA((3, features // chunk)),
        ],
        compiler_params=pltpu.CompilerParams(vmem_limit_bytes=56 << 20),
        cost_estimate=pl.CostEstimate(flops=1, bytes_accessed=1, transcendentals=0),
        name="project_rope",
    )(
        first_position, token, *[piece for half in pieces for piece in half],
        w_query, w_key, w_value, rope_rates(), *earlier,
    )


def attend_kernel(
    kv_heads, block, facts, packed_ref, kc_hbm, vc_hbm, kc_other, vc_other, out_ref, done_ref,
    kc_ref, vc_ref, m_ref, acc_ref, ve_ref, sems,
):
    done_ref[0] = 0
    span = packed_ref.shape[0]
    each = packed_ref.shape[1] // kv_heads
    groups = each // HD - 2
    slot, prefix, length, other = facts[0], facts[1], facts[2], facts[3]
    blocks = lax.div(prefix + (block - 1), block)
    factor = (HD**-0.5) * 1.4426950408889634
    contract = (((1,), (1,)), ((), ()))

    def copies(index, pair):
        piece = pl.ds(pl.multiple_of(index * block, block), block)
        return [
            pltpu.make_async_copy(source.at[slot, piece, :], target.at[piece, :], sems.at[n, index])
            for n, (source, target) in enumerate(zip(pair, (kc_ref, vc_ref)))
        ]

    def begin(index, carry):
        for wanted, pair in enumerate(((kc_hbm, vc_hbm), (kc_other, vc_other))):

            @pl.when(other == wanted)
            def _():
                for copy in copies(index, pair):
                    copy.start()

        return carry

    lax.fori_loop(0, blocks, begin, 0)
    ve_ref[:, HD:] = jnp.ones((ve_ref.shape[0], HD), jnp.bfloat16)
    row = lax.broadcasted_iota(jnp.int32, (span, span), 0)
    column = lax.broadcasted_iota(jnp.int32, (span, span), 1)
    keep_new = (column <= row) & (column < length)

    def scores_of(g, keys, keep):
        scores = []
        for m in range(groups):
            start = g * each + m * HD
            query = packed_ref[:, start : start + HD]
            score = lax.dot_general(query, keys, contract, preferred_element_type=jnp.float32)
            scores.append(jnp.where(keep, score * factor, masked))
        return scores

    for g in range(kv_heads):
        start = g * each + groups * HD
        scores = scores_of(g, packed_ref[:, start : start + HD], keep_new)
        ve_ref[:span, :HD] = packed_ref[:, start + HD : start + 2 * HD]
        tops = [jnp.max(score, axis=1, keepdims=True) for score in scores]
        weights = [
            jnp.exp2(score - top).astype(jnp.bfloat16) for score, top in zip(scores, tops)
        ]
        for m in range(groups):
            head = g * groups + m
            m_ref[head] = jnp.broadcast_to(tops[m], (span, HD))
            acc_ref[head] = jnp.dot(
                weights[m], ve_ref[:span, :], preferred_element_type=jnp.float32
            )

    def step(index, carry):
        for copy in copies(index, (kc_hbm, vc_hbm)):
            copy.wait()
        start = pl.multiple_of(index * block, block)
        piece = pl.ds(start, block)
        keep = (start + lax.broadcasted_iota(jnp.int32, (1, block), 1)) < prefix
        for g in range(kv_heads):
            here = slice(g * HD, (g + 1) * HD)
            scores = scores_of(g, kc_ref[piece, here], keep)
            ve_ref[:block, :HD] = vc_ref[piece, here]
            before = [m_ref[g * groups + m] for m in range(groups)]
            tops = [
                jnp.maximum(old, jnp.max(score, axis=1, keepdims=True))
                for old, score in zip(before, scores)
            ]
            weights = [
                jnp.exp2(score - top[:, :1]).astype(jnp.bfloat16)
                for score, top in zip(scores, tops)
            ]
            for m in range(groups):
                head = g * groups + m
                shrink = jnp.exp2(before[m] - tops[m])
                m_ref[head] = tops[m]
                acc_ref[head] = acc_ref[head] * jnp.concatenate([shrink, shrink], axis=1) + jnp.dot(
                    weights[m], ve_ref[:block, :], preferred_element_type=jnp.float32
                )
        return carry

    lax.fori_loop(0, blocks, step, 0)
    for head in range(kv_heads * groups):
        total = acc_ref[head]
        out_ref[:, head * HD : (head + 1) * HD] = (total[:, :HD] / total[:, HD:]).astype(
            out_ref.dtype
        )


def attend(facts, packed, cache_keys, cache_values, *others):
    span, width = packed.shape
    prefix, kv_width = cache_keys.shape[1:]
    kv_heads = kv_width // HD
    heads = width // HD - 2 * kv_heads
    block = min(1024, prefix)
    scalars = pl.BlockSpec(memory_space=pltpu.SMEM)
    here = pl.BlockSpec(memory_space=pltpu.VMEM)
    far_memory = pl.BlockSpec(memory_space=pltpu.HBM)
    return pl.pallas_call(
        functools.partial(attend_kernel, kv_heads, block),
        out_shape=[
            jax.ShapeDtypeStruct((span, heads * HD), jnp.bfloat16),
            jax.ShapeDtypeStruct((1,), jnp.int32),
        ],
        in_specs=[scalars, here] + [far_memory] * 4,
        out_specs=[here, scalars],
        scratch_shapes=[
            pltpu.VMEM((prefix, kv_width), jnp.bfloat16),
            pltpu.VMEM((prefix, kv_width), jnp.bfloat16),
            pltpu.VMEM((heads, span, HD), jnp.float32),
            pltpu.VMEM((heads, span, 2 * HD), jnp.float32),
            pltpu.VMEM((max(block, span), 2 * HD), jnp.bfloat16),
            pltpu.SemaphoreType.DMA((2, prefix // block)),
        ],
        compiler_params=pltpu.CompilerParams(vmem_limit_bytes=56 << 20),
        cost_estimate=pl.CostEstimate(flops=1, bytes_accessed=1, transcendentals=0),
        name="attend_slot",
    )(facts, packed, cache_keys, cache_values, *others)


def out_kernel(earlier, parts, line, tile, heads_ref, w_hbm, *refs):
    refs = refs[earlier:]
    outs = refs[:parts]
    firsts = refs[parts : 2 * parts] if line else ()
    done_ref, w_ref, sems = refs[-3:]
    done_ref[0] = 0
    columns = outs[0].shape[1]

    def copy(index):
        here = pl.ds(pl.multiple_of(index * tile, tile), tile)
        return pltpu.make_async_copy(w_hbm.at[:, here], w_ref.at[:, here], sems.at[index])

    def begin(index, carry):
        copy(index).start()
        return carry

    steps = columns // tile
    lax.fori_loop(0, parts * steps, begin, 0)
    if line:
        rows = firsts[0].shape[0]
        place = lax.axis_index("tensor")
        start = pl.multiple_of(jnp.where(place == 0, 3, 0) * rows, rows)
    for part in range(parts):

        def step(index, carry):
            copy(index + part * steps).wait()
            there = pl.ds(pl.multiple_of((index + part * steps) * tile, tile), tile)
            here = pl.ds(pl.multiple_of(index * tile, tile), tile)
            total = jnp.dot(heads_ref[...], w_ref[:, there], preferred_element_type=jnp.float32)
            outs[part][:, here] = total.astype(outs[part].dtype)
            return carry

        lax.fori_loop(0, steps, step, 0)
        if line:
            firsts[part][...] = outs[part][pl.ds(start, rows), :]


def out_columns(heads, w_out, parts, line, earlier=()):
    span = heads.shape[0]
    inputs, columns = w_out.shape
    width = columns // parts
    tile = min(512, width)
    here = pl.BlockSpec(memory_space=pltpu.VMEM)
    far_memory = pl.BlockSpec(memory_space=pltpu.HBM)
    shapes = [jax.ShapeDtypeStruct((span, width), jnp.bfloat16)] * parts
    if line:
        shapes += [jax.ShapeDtypeStruct((span // 4, width), jnp.bfloat16)] * parts
    results = pl.pallas_call(
        functools.partial(out_kernel, len(earlier), parts, line, tile),
        out_shape=shapes + [jax.ShapeDtypeStruct((1,), jnp.int32)],
        in_specs=[here] + [far_memory] * (1 + len(earlier)),
        out_specs=[here] * len(shapes) + [pl.BlockSpec(memory_space=pltpu.SMEM)],
        scratch_shapes=[
            pltpu.VMEM((inputs, columns), jnp.bfloat16),
            pltpu.SemaphoreType.DMA((columns // tile,)),
        ],
        compiler_params=pltpu.CompilerParams(vmem_limit_bytes=56 << 20),
        cost_estimate=pl.CostEstimate(flops=1, bytes_accessed=1, transcendentals=0),
        name="out_columns",
    )(heads, w_out, *earlier)
    return results[:parts], results[parts:-1], results[-1]


def add_rows(partial, index, rows, *received):
    mine = lax.dynamic_slice_in_dim(partial, index * rows, rows, 0)
    if not received:
        return mine
    total = mine.astype(jnp.float32)
    for other in received:
        total = total + other.astype(jnp.float32)
    return total.astype(jnp.bfloat16)


def zero_after(*arrays):
    total = jnp.zeros((1,), jnp.float32)
    for array in arrays:
        total = total + jnp.minimum(jnp.abs(array[:1, 0].astype(jnp.float32)), 0.0)
    return total.astype(jnp.int32)


def gather_first(own):
    up = lax.ppermute(own, "tensor", [(0, 1), (1, 2), (2, 3)])
    down = lax.ppermute(own, "tensor", [(1, 0), (2, 1), (3, 2)])
    return up, down


def gather_second(up, down):
    up_two = lax.ppermute(up, "tensor", [(1, 2), (2, 3)])
    down_two = lax.ppermute(down, "tensor", [(1, 0), (2, 1)])
    return up_two, down_two


def gather_third(up_two, down_two, place):
    held = jnp.where(place >= 2, up_two, down_two)
    return lax.ppermute(held, "tensor", [(2, 3), (1, 0)])


def sum_first(ends):
    return lax.ppermute(ends, "tensor", [(0, 1), (3, 2)])


def sum_second(partial, place, received):
    rows = partial.shape[0] // 4
    sent = add_rows(partial, jnp.where(place <= 1, place + 2, place - 2), rows, received)
    return (
        lax.ppermute(sent, "tensor", [(0, 1), (1, 2)]),
        lax.ppermute(sent, "tensor", [(3, 2), (2, 1)]),
    )


def sum_third(partial, place, up, down, token):
    rows = partial.shape[0] // 4
    place = place + token[0]
    sent_up = add_rows(partial, jnp.minimum(place + 1, 3), rows, up)
    sent_down = add_rows(partial, jnp.maximum(place - 1, 0), rows, down)
    return (
        lax.ppermute(sent_up, "tensor", [(0, 1), (1, 2), (2, 3)]),
        lax.ppermute(sent_down, "tensor", [(1, 0), (2, 1), (3, 2)]),
    )


def local(
    hidden_rows,
    norm_gain,
    w_query,
    w_key,
    w_value,
    w_out,
    cache_keys,
    cache_values,
    slot_of_request,
    span_length,
    prefix_length,
):
    data_size = lax.axis_size("dp")
    data_index = lax.axis_index("dp")
    tensor_size = lax.axis_size("tensor")
    place = lax.axis_index("tensor")
    rows, per_device, model = hidden_rows.shape
    span = rows * tensor_size
    q_width = w_query.shape[1]
    kv_width = w_key.shape[1]
    kv_heads = kv_width // HD
    line = tensor_size == 4
    cut = model // 2

    facts = find_facts(slot_of_request, span_length, prefix_length, per_device)
    far, far_mask = facts[0], facts[1]

    def by(bits):
        if bits == 0:
            return lambda values: values
        pairs = [(i, i ^ bits) for i in range(data_size)]
        return lambda values: lax.ppermute(values, "dp", pairs)

    nothing = jnp.zeros((1,), jnp.int32)
    swap = far == 1
    near_rows = jnp.where(swap, hidden_rows[:, 0, :], hidden_rows[:, 1, :])
    far_rows = jnp.where(swap, hidden_rows[:, 1, :], hidden_rows[:, 0, :])
    normed_near = normalize(near_rows, norm_gain)

    def caches_by(bits):
        def run(slot, *caches):
            lent = [lax.dynamic_index_in_dim(cache, slot, 0, True) for cache in caches]
            return [by(1)(cache) for cache in caches], [by(bits)(cache) for cache in lent]

        return run

    lending = facts[2], cache_keys, cache_values
    if line:

        def begin(bits):
            def run(rows, own, *lending):
                pieces = [own[:, c : c + cut] for c in (0, cut)]
                one = [gather_first(piece) for piece in pieces]
                caches = caches_by(bits)(*lending)
                two = [gather_second(*pair) for pair in one]
                three = [gather_third(*pair, place) for pair in two]
                gathered = [[p, *q, *r, t] for p, q, r, t in zip(pieces, one, two, three)]
                return gathered, normalize(rows, norm_gain), caches

            return run

        near_pieces, normed_far, (near_caches, far_caches) = lax.switch(
            lax.shift_right_logical(far_mask, 1),
            [begin(bits) for bits in range(0, data_size, 2)],
            far_rows,
            normed_near,
            *lending,
        )
        far_one = gather_first(normed_far)
    else:
        near_pieces = [[lax.all_gather(normed_near, "tensor", axis=0, tiled=True)]]
        near_caches, far_caches = lax.switch(
            lax.shift_right_logical(far_mask, 1),
            [caches_by(bits) for bits in range(0, data_size, 2)],
            *lending,
        )
        normed_far = normalize(far_rows, norm_gain)
        far_pieces = [[lax.all_gather(normed_far, "tensor", axis=0, tiled=True)]]
    weights = w_query, w_key, w_value
    packed, token = project(near_pieces, *weights, facts[4:5], nothing, span)
    heads, token = attend(facts[3:7], packed, *near_caches, *near_caches)
    if line:
        behind = token[0].astype(jnp.bfloat16)
        far_two = gather_second(*(piece + behind for piece in far_one))
    near_parts, near_ends, token = out_columns(heads, w_out, 1, line)
    earlier = []
    if line:
        near_one = sum_first(near_ends[0])
        far_three = gather_third(*far_two, place + token[0])
        far_pieces = [[normed_far, *far_one, *far_two, far_three]]
        near_two = sum_second(near_parts[0], place, near_one)
        earlier = [near_one]
    far_others = [by(1)(cache) for cache in far_caches]
    packed, token = project(far_pieces, *weights, facts[8:9], nothing, span, earlier)
    heads, token = attend(facts[7:11], packed, *far_caches, *far_others)
    if line:
        near_three = sum_third(near_parts[0], place, *near_two, token)
        far_parts, far_ends, _ = out_columns(heads, w_out, 2, line, near_two)
        far_one = [sum_first(ends) for ends in far_ends]
        behind = zero_after(*near_three)
        far_two = [sum_second(p, place + behind[0], q) for p, q in zip(far_parts, far_one)]
        far_three = [sum_third(p, place, *q, nothing) for p, q in zip(far_parts, far_two)]
        out_near = [add_rows(near_parts[0], place, rows, *near_three)]
        out_far = [add_rows(p, place, rows, *got) for p, got in zip(far_parts, far_three)]
    else:
        far_parts, _, _ = out_columns(heads, w_out, 1, line)
        out_near, out_far = [
            [lax.psum_scatter(part, "tensor", scatter_dimension=0, tiled=True) for part in parts]
            for parts in (near_parts, far_parts)
        ]
    out_near = jnp.concatenate(out_near, axis=1)
    out_far = jnp.concatenate(out_far, axis=1)
    return jnp.stack(
        [jnp.where(swap, out_near, out_far), jnp.where(swap, out_far, out_near)], axis=1
    )


def solution(mesh):
    placed = (
        P("tensor", "dp", None),
        P(),
        P(None, "tensor"),
        P(None, "tensor"),
        P(None, "tensor"),
        P("tensor", None),
        P("dp", None, "tensor"),
        P("dp", None, "tensor"),
        P(),
        P(),
        P(),
    )
    return jax.shard_map(
        local, mesh=mesh, in_specs=placed, out_specs=P("tensor", "dp", None), check_vma=False
    )
```

```python
import functools

import jax
import jax.numpy as jnp
from jax import lax
from jax.experimental import pallas as pl
from jax.experimental.pallas import tpu as pltpu
from jax.sharding import PartitionSpec as P

HD = 128
rope_base = 500000.0
norm_eps = 1e-05
masked = -1e30


def normalize(rows, norm_gain):
    floats = rows.astype(jnp.float32)
    return (
        floats * lax.rsqrt(jnp.mean(floats * floats, axis=-1, keepdims=True) + norm_eps) * norm_gain
    ).astype(jnp.bfloat16)


def rope_rates():
    half = HD // 2
    frequency = rope_base ** (-(jnp.arange(half, dtype=jnp.float32) * 2.0 / HD))
    return jnp.concatenate([frequency, frequency])[None, :]


def facts_kernel(per_device, slots_ref, spans_ref, prefixes_ref, out_ref):
    me = lax.axis_index("dp")
    base = me * per_device
    far = jnp.where(lax.div(slots_ref[base], per_device) ^ me == 1, 1, 0)
    far_mask = lax.div(slots_ref[base + far], per_device) ^ me
    host = (me ^ far_mask) * per_device
    guest = host + jnp.where(lax.div(slots_ref[host], per_device) == me, 0, 1)
    near = base + 1 - far
    out_ref[0] = far
    out_ref[1] = far_mask
    out_ref[2] = lax.rem(slots_ref[guest], per_device)
    out_ref[3] = lax.rem(slots_ref[near], per_device)
    out_ref[4] = prefixes_ref[near]
    out_ref[5] = spans_ref[near]
    out_ref[6] = 0
    out_ref[7] = 0
    out_ref[8] = prefixes_ref[base + far]
    out_ref[9] = spans_ref[base + far]
    out_ref[10] = far_mask & 1


def find_facts(slots, spans, prefixes, per_device):
    scalars = pl.BlockSpec(memory_space=pltpu.SMEM)
    return pl.pallas_call(
        functools.partial(facts_kernel, per_device),
        out_shape=jax.ShapeDtypeStruct((11,), jnp.int32),
        in_specs=[scalars] * 3,
        out_specs=scalars,
        name="find_facts",
    )(slots, spans, prefixes)


def project_kernel(chunk, kv_heads, groups, halves, sources, earlier, first_ref, token_ref, *refs):
    count = halves * sources
    pieces = [refs[h * sources : (h + 1) * sources] for h in range(halves)]
    wq_hbm, wk_hbm, wv_hbm, rates_ref = refs[count : count + 4]
    refs = refs[count + 4 + earlier :]
    out_ref, done_ref, x_ref, wq_ref, wk_ref, wv_ref, acc_ref, cos_ref, sin_ref, x_sems, sems = refs
    done_ref[0] = 0
    done_ref[0] = 0
    features = wq_hbm.shape[0]
    steps = features // chunk
    rows, width = pieces[0][0].shape
    place = lax.axis_index("tensor")

    def row_copies(half, act):
        columns = pl.ds(half * width, width)

        def copy(n, first):
            start = pl.multiple_of(first * rows, rows)
            act(
                pltpu.make_async_copy(
                    pieces[half][n], x_ref.at[pl.ds(start, pieces[half][n].shape[0]), columns],
                    x_sems.at[half, n],
                )
            )

        if sources == 1:
            copy(0, 0)
            return
        copy(0, place)
        for n, first, held in (
            (1, place - 1, place >= 1),
            (2, place + 1, place <= 2),
            (3, place - 2, place >= 2),
            (4, place + 2, place <= 1),
            (5, 3 - place, (place == 0) | (place == 3)),
        ):
            pl.when(held)(functools.partial(copy, n, first))

    def copies(index):
        piece = pl.ds(pl.multiple_of(index * chunk, chunk), chunk)
        return [
            pltpu.make_async_copy(source.at[piece, :], target.at[piece, :], sems.at[n, index])
            for n, (source, target) in enumerate(
                ((wq_hbm, wq_ref), (wk_hbm, wk_ref), (wv_hbm, wv_ref))
            )
        ]

    def begin(index, carry):
        for copy in copies(index):
            copy.start()
        return carry

    row_copies(0, lambda copy: copy.start())
    lax.fori_loop(0, 1, begin, 0)
    for half in range(1, halves):
        row_copies(half, lambda copy: copy.start())
    lax.fori_loop(1, steps, begin, 0)
    acc_ref[...] = jnp.zeros_like(acc_ref)
    row = lax.broadcasted_iota(jnp.int32, cos_ref.shape, 0)
    lane = lax.broadcasted_iota(jnp.int32, cos_ref.shape, 1)
    angles = (first_ref[0] + row).astype(jnp.float32) * rates_ref[...]
    cos_ref[...] = jnp.cos(angles)
    sin_ref[...] = jnp.where(lane < HD // 2, -1.0, 1.0) * jnp.sin(angles)

    def step(index, carry):
        for copy in copies(index):
            copy.wait()
        piece = pl.ds(pl.multiple_of(index * chunk, chunk), chunk)
        block = x_ref[:, piece]
        offset = 0
        for weights in (wq_ref, wk_ref, wv_ref):
            total = weights.shape[1]
            tile = min(256, total)
            for column in range(0, total, tile):
                acc_ref[:, offset + column : offset + column + tile] += jnp.dot(
                    block,
                    weights[piece, column : column + tile],
                    preferred_element_type=jnp.float32,
                )
            offset += total
        return carry

    each = steps // halves
    for half in range(halves):
        row_copies(half, lambda copy: copy.wait())
        lax.fori_loop(half * each, (half + 1) * each, step, 0)
    q_heads = kv_heads * groups
    for g in range(kv_heads):
        places = [g * groups + m for m in range(groups)] + [q_heads + g, q_heads + kv_heads + g]
        for slot, where in enumerate(places):
            part = acc_ref[:, where * HD : (where + 1) * HD]
            if slot <= groups:
                part = part * cos_ref[...] + pltpu.roll(part, HD // 2, 1) * sin_ref[...]
            start = (g * (groups + 2) + slot) * HD
            out_ref[:, start : start + HD] = part.astype(jnp.bfloat16)


def project(pieces, w_query, w_key, w_value, first_position, token, span, earlier=()):
    features = w_query.shape[0]
    q_width, kv_width = w_query.shape[1], w_key.shape[1]
    kv_heads, groups = kv_width // HD, q_width // kv_width
    halves, sources = len(pieces), len(pieces[0])
    chunk = min(1024, features // halves)
    width = q_width + 2 * kv_width
    far_memory = pl.BlockSpec(memory_space=pltpu.HBM)
    here = pl.BlockSpec(memory_space=pltpu.VMEM)
    return pl.pallas_call(
        functools.partial(project_kernel, chunk, kv_heads, groups, halves, sources, len(earlier)),
        out_shape=[
            jax.ShapeDtypeStruct((span, width), jnp.bfloat16),
            jax.ShapeDtypeStruct((1,), jnp.int32),
        ],
        in_specs=[pl.BlockSpec(memory_space=pltpu.SMEM)] * 2
        + [far_memory] * (halves * sources + 3)
        + [here]
        + [far_memory] * len(earlier),
        out_specs=[here, pl.BlockSpec(memory_space=pltpu.SMEM)],
        scratch_shapes=[
            pltpu.VMEM((span, features), jnp.bfloat16),
            pltpu.VMEM((features, q_width), jnp.bfloat16),
            pltpu.VMEM((features, kv_width), jnp.bfloat16),
            pltpu.VMEM((features, kv_width), jnp.bfloat16),
            pltpu.VMEM((span, width), jnp.float32),
            pltpu.VMEM((span, HD), jnp.float32),
            pltpu.VMEM((span, HD), jnp.float32),
            pltpu.SemaphoreType.DMA((halves, sources)),
            pltpu.SemaphoreType.DMA((3, features // chunk)),
        ],
        compiler_params=pltpu.CompilerParams(vmem_limit_bytes=56 << 20),
        cost_estimate=pl.CostEstimate(flops=1, bytes_accessed=1, transcendentals=0),
        name="project_rope",
    )(
        first_position, token, *[piece for half in pieces for piece in half],
        w_query, w_key, w_value, rope_rates(), *earlier,
    )


def attend_kernel(
    kv_heads, block, facts, packed_ref, kc_hbm, vc_hbm, kc_other, vc_other, out_ref, done_ref,
    kc_ref, vc_ref, m_ref, acc_ref, ve_ref, sems,
):
    done_ref[0] = 0
    span = packed_ref.shape[0]
    each = packed_ref.shape[1] // kv_heads
    groups = each // HD - 2
    slot, prefix, length, other = facts[0], facts[1], facts[2], facts[3]
    blocks = lax.div(prefix + (block - 1), block)
    factor = (HD**-0.5) * 1.4426950408889634
    contract = (((1,), (1,)), ((), ()))

    def copies(index, pair):
        piece = pl.ds(pl.multiple_of(index * block, block), block)
        return [
            pltpu.make_async_copy(source.at[slot, piece, :], target.at[piece, :], sems.at[n, index])
            for n, (source, target) in enumerate(zip(pair, (kc_ref, vc_ref)))
        ]

    def begin(index, carry):
        for wanted, pair in enumerate(((kc_hbm, vc_hbm), (kc_other, vc_other))):

            @pl.when(other == wanted)
            def _():
                for copy in copies(index, pair):
                    copy.start()

        return carry

    lax.fori_loop(0, blocks, begin, 0)
    ve_ref[:, HD:] = jnp.ones((ve_ref.shape[0], HD), jnp.bfloat16)
    row = lax.broadcasted_iota(jnp.int32, (span, span), 0)
    column = lax.broadcasted_iota(jnp.int32, (span, span), 1)
    keep_new = (column <= row) & (column < length)

    def scores_of(g, keys, keep):
        scores = []
        for m in range(groups):
            start = g * each + m * HD
            query = packed_ref[:, start : start + HD]
            score = lax.dot_general(query, keys, contract, preferred_element_type=jnp.float32)
            scores.append(jnp.where(keep, score * factor, masked))
        return scores

    for g in range(kv_heads):
        start = g * each + groups * HD
        scores = scores_of(g, packed_ref[:, start : start + HD], keep_new)
        ve_ref[:span, :HD] = packed_ref[:, start + HD : start + 2 * HD]
        tops = [jnp.max(score, axis=1, keepdims=True) for score in scores]
        weights = [
            jnp.exp2(score - top).astype(jnp.bfloat16) for score, top in zip(scores, tops)
        ]
        for m in range(groups):
            head = g * groups + m
            m_ref[head] = jnp.broadcast_to(tops[m], (span, HD))
            acc_ref[head] = jnp.dot(
                weights[m], ve_ref[:span, :], preferred_element_type=jnp.float32
            )

    def step(index, carry):
        for copy in copies(index, (kc_hbm, vc_hbm)):
            copy.wait()
        start = pl.multiple_of(index * block, block)
        piece = pl.ds(start, block)
        keep = (start + lax.broadcasted_iota(jnp.int32, (1, block), 1)) < prefix
        for g in range(kv_heads):
            here = slice(g * HD, (g + 1) * HD)
            scores = scores_of(g, kc_ref[piece, here], keep)
            ve_ref[:block, :HD] = vc_ref[piece, here]
            before = [m_ref[g * groups + m] for m in range(groups)]
            tops = [
                jnp.maximum(old, jnp.max(score, axis=1, keepdims=True))
                for old, score in zip(before, scores)
            ]
            weights = [
                jnp.exp2(score - top[:, :1]).astype(jnp.bfloat16)
                for score, top in zip(scores, tops)
            ]
            for m in range(groups):
                head = g * groups + m
                shrink = jnp.exp2(before[m] - tops[m])
                m_ref[head] = tops[m]
                acc_ref[head] = acc_ref[head] * jnp.concatenate([shrink, shrink], axis=1) + jnp.dot(
                    weights[m], ve_ref[:block, :], preferred_element_type=jnp.float32
                )
        return carry

    lax.fori_loop(0, blocks, step, 0)
    for head in range(kv_heads * groups):
        total = acc_ref[head]
        out_ref[:, head * HD : (head + 1) * HD] = (total[:, :HD] / total[:, HD:]).astype(
            out_ref.dtype
        )


def attend(facts, packed, cache_keys, cache_values, *others):
    span, width = packed.shape
    prefix, kv_width = cache_keys.shape[1:]
    kv_heads = kv_width // HD
    heads = width // HD - 2 * kv_heads
    block = min(1024, prefix)
    scalars = pl.BlockSpec(memory_space=pltpu.SMEM)
    here = pl.BlockSpec(memory_space=pltpu.VMEM)
    far_memory = pl.BlockSpec(memory_space=pltpu.HBM)
    return pl.pallas_call(
        functools.partial(attend_kernel, kv_heads, block),
        out_shape=[
            jax.ShapeDtypeStruct((span, heads * HD), jnp.bfloat16),
            jax.ShapeDtypeStruct((1,), jnp.int32),
        ],
        in_specs=[scalars, here] + [far_memory] * 4,
        out_specs=[here, scalars],
        scratch_shapes=[
            pltpu.VMEM((prefix, kv_width), jnp.bfloat16),
            pltpu.VMEM((prefix, kv_width), jnp.bfloat16),
            pltpu.VMEM((heads, span, HD), jnp.float32),
            pltpu.VMEM((heads, span, 2 * HD), jnp.float32),
            pltpu.VMEM((max(block, span), 2 * HD), jnp.bfloat16),
            pltpu.SemaphoreType.DMA((2, prefix // block)),
        ],
        compiler_params=pltpu.CompilerParams(vmem_limit_bytes=56 << 20),
        cost_estimate=pl.CostEstimate(flops=1, bytes_accessed=1, transcendentals=0),
        name="attend_slot",
    )(facts, packed, cache_keys, cache_values, *others)


def out_kernel(earlier, parts, line, tile, heads_ref, w_hbm, *refs):
    refs = refs[earlier:]
    outs = refs[:parts]
    firsts = refs[parts : 2 * parts] if line else ()
    done_ref, w_ref, sems = refs[-3:]
    done_ref[0] = 0
    columns = outs[0].shape[1]

    def copy(index):
        here = pl.ds(pl.multiple_of(index * tile, tile), tile)
        return pltpu.make_async_copy(w_hbm.at[:, here], w_ref.at[:, here], sems.at[index])

    def begin(index, carry):
        copy(index).start()
        return carry

    steps = columns // tile
    lax.fori_loop(0, parts * steps, begin, 0)
    if line:
        rows = firsts[0].shape[0]
        place = lax.axis_index("tensor")
        start = pl.multiple_of(jnp.where(place == 0, 3, 0) * rows, rows)
    for part in range(parts):

        def step(index, carry):
            copy(index + part * steps).wait()
            there = pl.ds(pl.multiple_of((index + part * steps) * tile, tile), tile)
            here = pl.ds(pl.multiple_of(index * tile, tile), tile)
            total = jnp.dot(heads_ref[...], w_ref[:, there], preferred_element_type=jnp.float32)
            outs[part][:, here] = total.astype(outs[part].dtype)
            return carry

        lax.fori_loop(0, steps, step, 0)
        if line:
            firsts[part][...] = outs[part][pl.ds(start, rows), :]


def out_columns(heads, w_out, parts, line, earlier=()):
    span = heads.shape[0]
    inputs, columns = w_out.shape
    width = columns // parts
    tile = min(1024, width)
    here = pl.BlockSpec(memory_space=pltpu.VMEM)
    far_memory = pl.BlockSpec(memory_space=pltpu.HBM)
    shapes = [jax.ShapeDtypeStruct((span, width), jnp.bfloat16)] * parts
    if line:
        shapes += [jax.ShapeDtypeStruct((span // 4, width), jnp.bfloat16)] * parts
    results = pl.pallas_call(
        functools.partial(out_kernel, len(earlier), parts, line, tile),
        out_shape=shapes + [jax.ShapeDtypeStruct((1,), jnp.int32)],
        in_specs=[here] + [far_memory] * (1 + len(earlier)),
        out_specs=[here] * len(shapes) + [pl.BlockSpec(memory_space=pltpu.SMEM)],
        scratch_shapes=[
            pltpu.VMEM((inputs, columns), jnp.bfloat16),
            pltpu.SemaphoreType.DMA((columns // tile,)),
        ],
        compiler_params=pltpu.CompilerParams(vmem_limit_bytes=56 << 20),
        cost_estimate=pl.CostEstimate(flops=1, bytes_accessed=1, transcendentals=0),
        name="out_columns",
    )(heads, w_out, *earlier)
    return results[:parts], results[parts:-1], results[-1]


def add_rows(partial, index, rows, *received):
    mine = lax.dynamic_slice_in_dim(partial, index * rows, rows, 0)
    if not received:
        return mine
    total = mine.astype(jnp.float32)
    for other in received:
        total = total + other.astype(jnp.float32)
    return total.astype(jnp.bfloat16)


def zero_after(*arrays):
    total = jnp.zeros((1,), jnp.float32)
    for array in arrays:
        total = total + jnp.minimum(jnp.abs(array[:1, 0].astype(jnp.float32)), 0.0)
    return total.astype(jnp.int32)


def gather_first(own):
    up = lax.ppermute(own, "tensor", [(0, 1), (1, 2), (2, 3)])
    down = lax.ppermute(own, "tensor", [(1, 0), (2, 1), (3, 2)])
    return up, down


def gather_second(up, down):
    up_two = lax.ppermute(up, "tensor", [(1, 2), (2, 3)])
    down_two = lax.ppermute(down, "tensor", [(1, 0), (2, 1)])
    return up_two, down_two


def gather_third(up_two, down_two, place):
    held = jnp.where(place >= 2, up_two, down_two)
    return lax.ppermute(held, "tensor", [(2, 3), (1, 0)])


def sum_first(ends):
    return lax.ppermute(ends, "tensor", [(0, 1), (3, 2)])


def sum_second(partial, place, received):
    rows = partial.shape[0] // 4
    sent = add_rows(partial, jnp.where(place <= 1, place + 2, place - 2), rows, received)
    return (
        lax.ppermute(sent, "tensor", [(0, 1), (1, 2)]),
        lax.ppermute(sent, "tensor", [(3, 2), (2, 1)]),
    )


def sum_third(partial, place, up, down, token):
    rows = partial.shape[0] // 4
    place = place + token[0]
    sent_up = add_rows(partial, jnp.minimum(place + 1, 3), rows, up)
    sent_down = add_rows(partial, jnp.maximum(place - 1, 0), rows, down)
    return (
        lax.ppermute(sent_up, "tensor", [(0, 1), (1, 2), (2, 3)]),
        lax.ppermute(sent_down, "tensor", [(1, 0), (2, 1), (3, 2)]),
    )


def local(
    hidden_rows,
    norm_gain,
    w_query,
    w_key,
    w_value,
    w_out,
    cache_keys,
    cache_values,
    slot_of_request,
    span_length,
    prefix_length,
):
    data_size = lax.axis_size("dp")
    data_index = lax.axis_index("dp")
    tensor_size = lax.axis_size("tensor")
    place = lax.axis_index("tensor")
    rows, per_device, model = hidden_rows.shape
    span = rows * tensor_size
    q_width = w_query.shape[1]
    kv_width = w_key.shape[1]
    kv_heads = kv_width // HD
    line = tensor_size == 4
    cut = model // 2

    facts = find_facts(slot_of_request, span_length, prefix_length, per_device)
    far, far_mask = facts[0], facts[1]

    def by(bits):
        if bits == 0:
            return lambda values: values
        pairs = [(i, i ^ bits) for i in range(data_size)]
        return lambda values: lax.ppermute(values, "dp", pairs)

    nothing = jnp.zeros((1,), jnp.int32)
    swap = far == 1
    near_rows = jnp.where(swap, hidden_rows[:, 0, :], hidden_rows[:, 1, :])
    far_rows = jnp.where(swap, hidden_rows[:, 1, :], hidden_rows[:, 0, :])
    normed_near = normalize(near_rows, norm_gain)

    def caches_by(bits):
        def run(slot, *caches):
            lent = [lax.dynamic_index_in_dim(cache, slot, 0, True) for cache in caches]
            return [by(1)(cache) for cache in caches], [by(bits)(cache) for cache in lent]

        return run

    lending = facts[2], cache_keys, cache_values
    if line:

        def begin(bits):
            def run(rows, own, *lending):
                pieces = [own[:, c : c + cut] for c in (0, cut)]
                one = [gather_first(piece) for piece in pieces]
                caches = caches_by(bits)(*lending)
                two = [gather_second(*pair) for pair in one]
                three = [gather_third(*pair, place) for pair in two]
                gathered = [[p, *q, *r, t] for p, q, r, t in zip(pieces, one, two, three)]
                return gathered, normalize(rows, norm_gain), caches

            return run

        near_pieces, normed_far, (near_caches, far_caches) = lax.switch(
            lax.shift_right_logical(far_mask, 1),
            [begin(bits) for bits in range(0, data_size, 2)],
            far_rows,
            normed_near,
            *lending,
        )
        far_one = gather_first(normed_far)
    else:
        near_pieces = [[lax.all_gather(normed_near, "tensor", axis=0, tiled=True)]]
        near_caches, far_caches = lax.switch(
            lax.shift_right_logical(far_mask, 1),
            [caches_by(bits) for bits in range(0, data_size, 2)],
            *lending,
        )
        normed_far = normalize(far_rows, norm_gain)
        far_pieces = [[lax.all_gather(normed_far, "tensor", axis=0, tiled=True)]]
    weights = w_query, w_key, w_value
    packed, token = project(near_pieces, *weights, facts[4:5], nothing, span)
    heads, token = attend(facts[3:7], packed, *near_caches, *near_caches)
    if line:
        behind = token[0].astype(jnp.bfloat16)
        far_two = gather_second(*(piece + behind for piece in far_one))
    near_parts, near_ends, token = out_columns(heads, w_out, 1, line)
    earlier = []
    if line:
        near_one = sum_first(near_ends[0])
        far_three = gather_third(*far_two, place + token[0])
        far_pieces = [[normed_far, *far_one, *far_two, far_three]]
        near_two = sum_second(near_parts[0], place, near_one)
        earlier = [near_one]
    far_others = [by(1)(cache) for cache in far_caches]
    packed, token = project(far_pieces, *weights, facts[8:9], nothing, span, earlier)
    heads, token = attend(facts[7:11], packed, *far_caches, *far_others)
    if line:
        near_three = sum_third(near_parts[0], place, *near_two, token)
        far_parts, far_ends, _ = out_columns(heads, w_out, 2, line, near_two)
        far_one = [sum_first(ends) for ends in far_ends]
        behind = zero_after(*near_three)
        far_two = [sum_second(p, place + behind[0], q) for p, q in zip(far_parts, far_one)]
        far_three = [sum_third(p, place, *q, nothing) for p, q in zip(far_parts, far_two)]
        out_near = [add_rows(near_parts[0], place, rows, *near_three)]
        out_far = [add_rows(p, place, rows, *got) for p, got in zip(far_parts, far_three)]
    else:
        far_parts, _, _ = out_columns(heads, w_out, 1, line)
        out_near, out_far = [
            [lax.psum_scatter(part, "tensor", scatter_dimension=0, tiled=True) for part in parts]
            for parts in (near_parts, far_parts)
        ]
    out_near = jnp.concatenate(out_near, axis=1)
    out_far = jnp.concatenate(out_far, axis=1)
    return jnp.stack(
        [jnp.where(swap, out_near, out_far), jnp.where(swap, out_far, out_near)], axis=1
    )


def solution(mesh):
    placed = (
        P("tensor", "dp", None),
        P(),
        P(None, "tensor"),
        P(None, "tensor"),
        P(None, "tensor"),
        P("tensor", None),
        P("dp", None, "tensor"),
        P("dp", None, "tensor"),
        P(),
        P(),
        P(),
    )
    return jax.shard_map(
        local, mesh=mesh, in_specs=placed, out_specs=P("tensor", "dp", None), check_vma=False
    )
```
